256 devices in a mesh: frame: 32 (over y, z), head: 8 (over x, core).
Axes of the slice: x: 4, y: 4, z: 8, core: 2. Of those that a mesh axis runs over, the one named last changes fastest.
Arguments:
- queries: bfloat16 [32768, 5120], P('frame', 'head'), may hold values from -120 to 120
- key_states: bfloat16 [32768, 5120], P('frame', 'head'), may hold values from -6 to 6
- value_states: bfloat16 [32768, 5120], P('frame', 'head'), may hold values from -6 to 6
- out_weight: bfloat16 [5120, 5120], P('frame', 'head'), may hold values from -0.078125 to 0.078125
- head_labels: int32 [40], replicated, may hold values from 0 to 1, as said below
Outputs:
- projected: bfloat16 [32768, 5120], P('frame', 'head')
The draws below stay inside these ranges and needn't reach their ends.
Inputs may be any that keep to these rules, and one draw needn't show every extreme that they name: `head_labels`: every 5 heads in a row (heads g * 5 to g * 5 + 4) hold 3 or 2 temporal heads; some such group holds 3, some other 2.
All inputs are finite; a program needn't handle non-finite values.
Results may differ from the reference program's by a relative error of at most 0.015.
Values may be sent and summed in bfloat16 or wider, within the bound.
A program may use at most 128 MiB of HBM per device.

```python
import jax
import jax.numpy as jnp
from jax import lax

D = 5120
HEADS = 40
HDIM = 128
POS = 1024
FRAMES = 32
HD = 5120
HEAD_DEV = 5
TMAX = 3


def shared_keys(key):
    return jnp.clip(jax.random.normal(key, (FRAMES * POS, HEADS * HDIM), jnp.float32), -6.0, 6.0)


def draw_key_states(key, part):
    base = shared_keys(key)
    return base.astype(jnp.bfloat16)


def draw_queries(key, part):
    key = jax.random.fold_in(key, 7)
    values = jnp.clip(jax.random.normal(key, (FRAMES * POS, HEADS * HDIM), jnp.float32), -6.0, 6.0)
    return values.astype(jnp.bfloat16)


def draw_head_labels(key, part):
    key = jax.random.fold_in(key, 11)
    groups = HEADS // HEAD_DEV
    key_a, key_b, key_c, key_d = jax.random.split(key, 4)
    counts = TMAX - 1 + jax.random.randint(key_a, (groups,), 0, 2)
    first = jax.random.randint(key_b, (), 0, groups)
    second = (first + 1 + jax.random.randint(key_c, (), 0, groups - 1)) % groups
    counts = counts.at[first].set(TMAX).at[second].set(TMAX - 1)
    ranks = jax.vmap(lambda single: jax.random.permutation(single, HEAD_DEV))(jax.random.split(key_d, groups))
    return (ranks < counts[:, None]).astype(jnp.int32).reshape(HEADS)


def levels(key, dims, pieces, least, high):
    def one(axis_at, blocks):
        heights = jax.random.uniform(jax.random.fold_in(jax.random.fold_in(key, 6), axis_at), (blocks,), jnp.float32, least / len(pieces), high / len(pieces))
        return jnp.repeat(jnp.exp(heights), dims[axis_at] // blocks).reshape((-1,) + (1,) * (len(dims) - axis_at - 1))

    factor_of = one(*pieces[0])
    for cut in pieces[1:]:
        factor_of = factor_of * one(*cut)
    return factor_of


def gaussian(own_key, extent, deviation, reach, pieces=(), kind=jnp.bfloat16):
    array = deviation * jax.random.normal(own_key, extent, jnp.float32)
    if pieces:
        array = array * levels(own_key, extent, pieces, -0.22, 0.18)
    return jnp.clip(array, -reach, reach).astype(kind)


def setup_inputs(seed: int = 0) -> dict:
    arg_keys = jax.random.split(jax.random.key(seed), 6)
    queries = draw_queries(jax.random.fold_in(arg_keys[5], 71), 0)
    key_states = draw_key_states(jax.random.fold_in(arg_keys[5], 71), 0)
    value_states = gaussian(arg_keys[2], (FRAMES * POS, HD), 1.0, 6.0, ((0, 32), (1, 8)))
    out_weight = gaussian(arg_keys[3], (HD, D), HD ** -0.5, 0.078125, ((0, 32), (1, 8)))
    head_labels = draw_head_labels(jax.random.fold_in(arg_keys[5], 71), 0)
    return {"queries": queries, "key_states": key_states, "value_states": value_states, "out_weight": out_weight, "head_labels": head_labels}


def attend_heads(query_rows, key_rows, value_rows):
    scale = query_rows.shape[-1] ** -0.5
    scores = jnp.einsum('rld,rmd->rlm', query_rows.astype(jnp.float32), key_rows.astype(jnp.float32)) * scale
    largest = jnp.max(scores, axis=-1, keepdims=True)
    expo = jnp.exp(scores - largest)
    weights = (expo / jnp.sum(expo, axis=-1, keepdims=True)).astype(jnp.bfloat16)
    mixed_output = jnp.einsum('rlm,rmd->rld', weights.astype(jnp.float32), value_rows.astype(jnp.float32))
    return mixed_output.astype(jnp.bfloat16)


def reference(queries, key_states, value_states, out_weight, head_labels):
    query_heads = queries.reshape(FRAMES, POS, HEADS, HDIM)
    key_heads = key_states.reshape(FRAMES, POS, HEADS, HDIM)
    value_per_head = value_states.reshape(FRAMES, POS, HEADS, HDIM)

    def one_head(head_index):
        selected_queries = lax.dynamic_index_in_dim(query_heads, head_index, 2, keepdims=False)
        selected_keys = lax.dynamic_index_in_dim(key_heads, head_index, 2, keepdims=False)
        selected_values = lax.dynamic_index_in_dim(value_per_head, head_index, 2, keepdims=False)

        def spatial():
            return lax.map(lambda query_key_value: attend_heads(query_key_value[0][None], query_key_value[1][None], query_key_value[2][None])[0], (selected_queries, selected_keys, selected_values))

        def temporal():
            mixed_output = attend_heads(selected_queries.transpose(1, 0, 2), selected_keys.transpose(1, 0, 2), selected_values.transpose(1, 0, 2))
            return mixed_output.transpose(1, 0, 2)

        return lax.cond(head_labels[head_index] == 1, temporal, spatial)

    heads_out = lax.map(one_head, jnp.arange(HEADS, dtype=jnp.int32))
    attended = heads_out.transpose(1, 2, 0, 3).reshape(FRAMES * POS, HEADS * HDIM)
    return jnp.dot(attended, out_weight, preferred_element_type=jnp.float32).astype(jnp.bfloat16)
```

```python
import functools
import math

import jax
import jax.numpy as jnp
from jax import lax
from jax.experimental import pallas as pl
from jax.experimental.pallas import tpu as pltpu
from jax.sharding import PartitionSpec as P

MESH = pl.DeviceIdType.MESH
BF16 = jnp.bfloat16
F32 = jnp.float32
HDIM = 128
POS = 1024
FRAMES = 32
NY, NZ, NX = 4, 8, 4
GROUPS = 8
HEAD_DEV = 5
PB = POS // FRAMES
WROWS = 160
COLS = 640
EXP_SCALE = HDIM**-0.5 * math.log2(math.e)
NEG = -1e30

SLOT_EITHER = 2
SENT = (2, 3, 4)


def wait_on(ref, sem):
    pltpu.make_async_copy(ref, ref, sem).wait()


def remote(src, dst, send_sem, recv_sem, device):
    return pltpu.make_async_remote_copy(
        src_ref=src,
        dst_ref=dst,
        send_sem=send_sem,
        recv_sem=recv_sem,
        device_id=device,
        device_id_type=MESH,
    )


def frame_rows(frame):
    return pl.ds(pl.multiple_of(frame * PB, PB), PB)


def partner(k, y, z):
    turn = (k * 11) % FRAMES
    return ((y + turn // NZ) % NY) * NZ + (z + turn % NZ) % NZ


class WeightRing:
    def __init__(self, rows, zs, zr, ys, yr, head, y, z):
        self.rows, self.zs, self.zr, self.ys, self.yr = rows, zs, zr, ys, yr
        self.y, self.z = y, z
        self.z_next = (y * NZ + (z + 1) % NZ, head)
        self.z_prev = (y * NZ + (z + NZ - 1) % NZ, head)
        self.y_next = (((y + 1) % NY) * NZ + z, head)
        self.y_prev = (((y + NY - 1) % NY) * NZ + z, head)

    def block(self, y, z, half=None):
        row = ((y % NY) * NZ + z % NZ) * WROWS
        if half is None:
            return self.rows.at[pl.ds(row // 16, WROWS // 16)]
        return self.rows.at[pl.ds(row // 16 + half * 5, 5)]

    def send_z(self, t):
        up = self.block(self.y, self.z + NZ + 1 - t, None if t < 4 else 0)
        down = self.block(self.y, self.z + t - 1, None if t < 4 else 1)
        remote(up, up, self.zs.at[0, t - 1], self.zr.at[0, t - 1], self.z_next).start()
        remote(down, down, self.zs.at[1, t - 1], self.zr.at[1, t - 1], self.z_prev).start()

    def wait_z(self, t):
        wait_on(self.block(self.y, self.z + NZ - t, None if t < 4 else 0), self.zr.at[0, t - 1])
        wait_on(self.block(self.y, self.z + t, None if t < 4 else 1), self.zr.at[1, t - 1])

    def send_y(self, dz):
        own = self.block(self.y, self.z + dz)
        remote(own, own, self.ys.at[0, dz], self.yr.at[0, dz], self.y_next).start()
        remote(own, own, self.ys.at[1, dz], self.yr.at[1, dz], self.y_prev).start()

    def relay_y(self, dz):
        wait_on(self.block(self.y + NY - 1, self.z + dz), self.yr.at[0, dz])
        low = self.block(self.y + NY - 1, self.z + dz, 0)
        remote(low, low, self.ys.at[2, dz], self.yr.at[2, dz], self.y_next).start()
        wait_on(self.block(self.y + 1, self.z + dz), self.yr.at[1, dz])
        high = self.block(self.y + 1, self.z + dz, 1)
        remote(high, high, self.ys.at[3, dz], self.yr.at[3, dz], self.y_prev).start()

    def finish_y(self, dz):
        wait_on(self.block(self.y + 2, self.z + dz, 0), self.yr.at[2, dz])
        wait_on(self.block(self.y + 2, self.z + dz, 1), self.yr.at[3, dz])

    def drain(self):
        whole, half = self.block(self.y, self.z), self.block(self.y, self.z, 0)
        for t in range(1, 5):
            for way in range(2):
                wait_on(whole if t < 4 else half, self.zs.at[way, t - 1])
        for dz in range(NZ):
            for way in range(4):
                wait_on(whole if way < 2 else half, self.ys.at[way, dz])


class AttendedRing:
    def __init__(self, groups, send, recv, frame, x, core):
        self.groups, self.send, self.recv = groups, send, recv
        self.x, self.core = x, core
        self.next = (frame, ((x + 1) % NX) * 2 + core)
        self.prev = (frame, ((x + NX - 1) % NX) * 2 + core)
        self.other = (frame, x * 2 + 1 - core)

    def whole(self, x, core):
        return self.groups.at[(x % NX) * 2 + core]

    def half(self, x, core, k):
        return self.groups.at[(x % NX) * 2 + core, pl.ds(k * 512, 512), :]

    def copy(self, ref, k, device):
        remote(ref, ref, self.send.at[k], self.recv.at[k], device).start()

    def own(self):
        mine = self.whole(self.x, self.core)
        self.copy(mine, 0, self.next)
        self.copy(mine, 1, self.prev)
        self.copy(mine, 2, self.other)

    def relay(self):
        came = self.whole(self.x + NX - 1, self.core)
        wait_on(came, self.recv.at[0])
        self.copy(self.half(self.x + NX - 1, self.core, 0), 3, self.next)
        self.copy(came, 5, self.other)
        came = self.whole(self.x + 1, self.core)
        wait_on(came, self.recv.at[1])
        self.copy(self.half(self.x + 1, self.core, 1), 4, self.prev)
        self.copy(came, 6, self.other)

    def relay_far(self):
        for k in range(2):
            came = self.half(self.x + 2, self.core, k)
            wait_on(came, self.recv.at[3 + k])
            self.copy(came, 7 + k, self.other)

    def finish(self):
        across = 1 - self.core
        wait_on(self.whole(self.x, across), self.recv.at[2])
        wait_on(self.whole(self.x + NX - 1, across), self.recv.at[5])
        wait_on(self.whole(self.x + 1, across), self.recv.at[6])
        wait_on(self.half(self.x + 2, across, 0), self.recv.at[7])
        wait_on(self.half(self.x + 2, across, 1), self.recv.at[8])

    def drain(self):
        whole, half = self.whole(self.x, self.core), self.half(self.x, self.core, 0)
        for k in (0, 1, 2, 5, 6):
            wait_on(whole, self.send.at[k])
        for k in (3, 4, 7, 8):
            wait_on(half, self.send.at[k])


def softmax_rows(scores):
    largest = jnp.max(scores, axis=-1, keepdims=True)
    expo = jnp.exp2((scores - largest) * EXP_SCALE)
    return expo.astype(BF16), jnp.sum(expo, axis=-1, keepdims=True)


def dot_t(a, b):
    return lax.dot_general(a, b, (((1,), (1,)), ((), ())), preferred_element_type=F32)


def block_kernel(
    info,
    q_hbm,
    k_hbm,
    v_hbm,
    w_hbm,
    out,
    heads_in,
    slots,
    got,
    mixed,
    either_spatial,
    either_temporal,
    gathered,
    weight,
    picked_weight,
    total,
    load_sem,
    fwd_send,
    fwd_recv,
    ret_send,
    ret_recv,
    wz_send,
    wz_recv,
    wy_send,
    wy_recv,
    x_send,
    x_recv,
):
    frame, head = lax.axis_index("frame"), lax.axis_index("head")
    y, z = frame // NZ, frame % NZ
    x, core = head // 2, head % 2

    loads = [
        pltpu.make_async_copy(
            source.at[:, pl.ds(h * HDIM, HDIM)], heads_in.at[n, h], load_sem.at[n, h]
        )
        for n, source in enumerate((q_hbm, k_hbm, v_hbm))
        for h in range(HEAD_DEV)
    ]
    loads += [
        pltpu.make_async_copy(
            w_hbm.at[pl.ds(n * 16, 16), :], weight.at[frame * 10 + n], load_sem.at[3, n]
        )
        for n in range(10)
    ]
    for load in loads:
        load.start()

    barrier = pltpu.get_barrier_semaphore()

    def greet(k, carry):
        pl.semaphore_signal(
            barrier, inc=1, device_id=((frame + k) % FRAMES, head), device_id_type=MESH
        )
        return carry

    lax.fori_loop(1, FRAMES, greet, 0)
    for there in (((x + 1) % NX) * 2 + core, ((x + NX - 1) % NX) * 2 + core, x * 2 + 1 - core):
        pl.semaphore_signal(barrier, inc=1, device_id=(frame, there), device_id_type=MESH)

    for load in loads:
        load.wait()
    for slot in range(HEAD_DEV):
        for n in range(3):
            slots[slot, n] = heads_in[n, info[head * 8 + slot]]

    pl.semaphore_wait(barrier, FRAMES - 1 + 3)

    ring = WeightRing(weight, wz_send, wz_recv, wy_send, wy_recv, head, y, z)
    gather = [
        AttendedRing(gathered.at[slot], x_send.at[slot], x_recv.at[slot], frame, x, core)
        for slot in range(HEAD_DEV)
    ]

    def send_forward(s):
        def one(k, carry):
            to = partner(k, y, z)
            remote(
                slots.at[SENT[s], :, frame_rows(to), :],
                got.at[s, :, frame_rows(frame), :],
                fwd_send.at[s],
                fwd_recv.at[s],
                (to, head),
            ).start()
            return carry

        lax.fori_loop(1, FRAMES, one, 0)
        pltpu.make_async_copy(
            slots.at[SENT[s], :, frame_rows(frame), :],
            got.at[s, :, frame_rows(frame), :],
            fwd_recv.at[s],
        ).start()

    def returned(s):
        return either_temporal if SENT[s] == SLOT_EITHER else gathered.at[SENT[s], head]

    def send_back(s):
        def one(k, carry):
            to = partner(k, y, z)
            remote(
                mixed.at[s, frame_rows(to), :],
                returned(s).at[frame_rows(frame), :],
                ret_send.at[s],
                ret_recv.at[s],
                (to, head),
            ).start()
            return carry

        lax.fori_loop(1, FRAMES, one, 0)
        pltpu.make_async_copy(
            mixed.at[s, frame_rows(frame), :],
            returned(s).at[frame_rows(frame), :],
            ret_recv.at[s],
        ).start()

    def spatial(slot, dest):
        def one(i, carry):
            rows = pl.ds(pl.multiple_of(i * 256, 256), 256)
            expo, row_sum = softmax_rows(dot_t(slots[slot, 0, rows, :], slots[slot, 1]))
            mix = jnp.dot(expo, slots[slot, 2], preferred_element_type=F32)
            dest[rows, :] = (mix / row_sum).astype(BF16)
            return carry

        lax.fori_loop(0, POS // 256, one, 0)

    def temporal(s):
        wait_on(got.at[s], fwd_recv.at[s])
        row_at = lax.broadcasted_iota(jnp.int32, (512, 512), 0) % 16
        col_at = lax.broadcasted_iota(jnp.int32, (512, 512), 1) % 16
        same = row_at == col_at
        for half in range(2):
            query, key, value = (
                got[s, n].reshape(FRAMES, 2, 16, HDIM)[:, half].reshape(512, HDIM)
                for n in range(3)
            )
            expo, row_sum = softmax_rows(jnp.where(same, dot_t(query, key), NEG))
            mix = jnp.dot(expo, value, preferred_element_type=F32)
            mix = (mix / row_sum).astype(BF16).reshape(FRAMES, 16, HDIM)
            for f in range(FRAMES):
                mixed[s, pl.ds(f * PB + half * 16, 16), :] = mix[f]

    def project(slot, first, last):
        for g in range(GROUPS):
            at = (info[g * 8 + slot] + g * HEAD_DEV) * 8
            for n in range(8):
                picked_weight[pl.ds(g * HDIM + n * 16, 16), :] = weight[at + n]

        def one(i, carry):
            rows = pl.ds(pl.multiple_of(i * 256, 256), 256)
            left = jnp.concatenate([gathered[slot, g, rows, :] for g in range(GROUPS)], axis=1)
            part = jnp.dot(left, picked_weight[...], preferred_element_type=F32)
            if not first:
                part = part + total[rows, :]
            if last:
                out[rows, :] = part.astype(BF16)
            else:
                total[rows, :] = part
            return carry

        lax.fori_loop(0, POS // 256, one, 0)

    ring.send_z(1)
    ring.send_y(0)
    send_forward(0)
    spatial(0, gathered.at[0, head])
    gather[0].own()
    ring.wait_z(1)
    ring.send_z(2)
    ring.send_y(1)
    ring.send_y(7)
    send_forward(1)
    spatial(1, gathered.at[1, head])
    gather[1].own()
    ring.wait_z(2)
    ring.send_z(3)
    ring.send_y(2)
    ring.send_y(6)
    ring.relay_y(0)
    send_forward(2)
    spatial(SLOT_EITHER, either_spatial)
    gather[0].relay()
    ring.wait_z(3)
    ring.send_z(4)
    ring.send_y(3)
    ring.send_y(5)
    ring.relay_y(1)
    ring.relay_y(7)
    gather[0].relay_far()
    temporal(0)
    send_back(0)
    ring.wait_z(4)
    ring.send_y(4)
    ring.relay_y(2)
    ring.relay_y(6)
    gather[1].relay()
    gather[1].relay_far()
    temporal(1)
    send_back(1)
    ring.relay_y(3)
    ring.relay_y(5)

    wait_on(either_temporal, ret_recv.at[0])
    is_temporal = jnp.full((POS, HDIM), info[head * 8 + HEAD_DEV], jnp.int32) == 1
    gathered[SLOT_EITHER, head] = jnp.where(
        is_temporal, either_temporal[...], either_spatial[...]
    )
    gather[2].own()
    temporal(2)
    send_back(2)
    ring.relay_y(4)
    wait_on(returned(1), ret_recv.at[1])
    gather[3].own()
    gather[2].relay()
    gather[2].relay_far()
    for dz in range(NZ):
        ring.finish_y(dz)
    gather[0].finish()
    project(0, True, False)
    gather[3].relay()
    wait_on(returned(2), ret_recv.at[2])
    gather[4].own()
    gather[3].relay_far()
    gather[1].finish()
    project(1, False, False)
    gather[4].relay()
    gather[2].finish()
    project(2, False, False)
    gather[4].relay_far()
    gather[3].finish()
    project(3, False, False)
    gather[4].finish()
    project(4, False, True)

    ring.drain()
    for each in gather:
        each.drain()
    for s in range(3):
        wait_on(slots.at[SENT[s], :, pl.ds(0, POS - PB), :], fwd_send.at[s])
        wait_on(mixed.at[s, pl.ds(0, POS - PB), :], ret_send.at[s])


def slot_table(head_labels):
    labels = head_labels.reshape(GROUPS, HEAD_DEV)
    spatial = 1 - labels
    n_spatial = jnp.sum(spatial, axis=1, keepdims=True)
    rank = jnp.where(
        labels == 0,
        jnp.cumsum(spatial, axis=1) - 1,
        n_spatial + jnp.cumsum(labels, axis=1) - 1,
    )
    at = jnp.arange(HEAD_DEV, dtype=jnp.int32)
    heads = jnp.sum(jnp.where(rank[:, :, None] == at, at[None, :, None], 0), axis=1)
    table = jnp.concatenate(
        [heads, (n_spatial == 2).astype(jnp.int32), jnp.zeros((GROUPS, 2), jnp.int32)], axis=1
    )
    return table.reshape(GROUPS * 8)


def per_device(queries, key_states, value_states, out_weight, head_labels):
    any_spec = pl.BlockSpec(memory_space=pl.ANY)
    dma = pltpu.SemaphoreType.DMA
    return pl.pallas_call(
        block_kernel,
        out_shape=jax.ShapeDtypeStruct((POS, COLS), BF16),
        in_specs=[pl.BlockSpec(memory_space=pltpu.SMEM)] + [any_spec] * 4,
        out_specs=pl.BlockSpec(memory_space=pltpu.VMEM),
        scratch_shapes=[
            pltpu.VMEM((3, HEAD_DEV, POS, HDIM), BF16),
            pltpu.VMEM((HEAD_DEV, 3, POS, HDIM), BF16),
            pltpu.VMEM((3, 3, POS, HDIM), BF16),
            pltpu.VMEM((3, POS, HDIM), BF16),
            pltpu.VMEM((POS, HDIM), BF16),
            pltpu.VMEM((POS, HDIM), BF16),
            pltpu.VMEM((HEAD_DEV, GROUPS, POS, HDIM), BF16),
            pltpu.VMEM((WROWS * FRAMES // 16, 16, COLS), BF16),
            pltpu.VMEM((GROUPS * HDIM, COLS), BF16),
            pltpu.VMEM((POS, COLS), F32),
            dma((4, 10)),
            dma((3,)),
            dma((3,)),
            dma((3,)),
            dma((3,)),
            dma((2, 4)),
            dma((2, 4)),
            dma((4, NZ)),
            dma((4, NZ)),
            dma((HEAD_DEV, 9)),
            dma((HEAD_DEV, 9)),
        ],
        compiler_params=pltpu.CompilerParams(
            collective_id=0, has_side_effects=True, vmem_limit_bytes=56 << 20
        ),
        name="block_kernel",
    )(slot_table(head_labels), queries, key_states, value_states, out_weight)


def solution(mesh):
    return jax.shard_map(
        per_device,
        mesh=mesh,
        in_specs=(
            P("frame", "head"),
            P("frame", "head"),
            P("frame", "head"),
            P("frame", "head"),
            P(),
        ),
        out_specs=P("frame", "head"),
        check_vma=False,
    )
```

```python
import functools
import math

import jax
import jax.numpy as jnp
from jax import lax
from jax.experimental import pallas as pl
from jax.experimental.pallas import tpu as pltpu
from jax.sharding import PartitionSpec as P

MESH = pl.DeviceIdType.MESH
BF16 = jnp.bfloat16
F32 = jnp.float32
HDIM = 128
POS = 1024
FRAMES = 32
NY, NZ, NX = 4, 8, 4
GROUPS = 8
HEAD_DEV = 5
PB = POS // FRAMES
WROWS = 160
COLS = 640
EXP_SCALE = HDIM**-0.5 * math.log2(math.e)
NEG = -1e30
HALF = PB // 2
TILED = (FRAMES, 2, HALF, HDIM)

SLOT_EITHER = 2
SENT = (2, 3, 4)

ORDER = (
    ("zs", 1), ("ys", 0), ("pick", 2), ("fwd", 0, 0), ("fwd", 0, 1), ("pick", 0), ("pick", 1), ("pick", 3),
    ("pick", 4), ("zw", 1), ("zs", 2), ("ys", 1), ("ys", 7), ("fwd", 0, 2), ("fwd", 0, 3), ("sp", 0),
    ("xo", 0), ("yr", 0), ("zw", 2), ("ys", 2), ("ys", 6), ("fwd", 1, 0), ("fwd", 1, 1), ("zs", 3),
    ("fwd", 1, 2), ("fwd", 1, 3), ("sp", 1), ("xo", 1), ("yr", 1), ("yr", 7), ("tm", 0), ("sp", 2), ("xr", 0),
    ("xf", 0), ("yr", 2), ("yr", 6), ("zw", 3), ("zs", 4), ("ys", 3), ("ys", 5), ("fwh", 0, 0), ("back", 0),
    ("xo", 2), ("xr", 1), ("xf", 1), ("tm", 1), ("fwh", 0, 1), ("xr", 2), ("zw", 4), ("ys", 4), ("fwh", 1, 0),
    ("fwh", 1, 1), ("yr", 3), ("yr", 5), ("xf", 2), ("xe", 0), ("xe", 1), ("mm", 0), ("xe", 2), ("back", 1),
    ("xo", 3), ("yr", 4), ("mm", 1), ("tmh", 0), ("xr", 3), ("mm", 2), ("tmh", 1), ("mm", 3), ("xf", 3),
    ("bkh", 0), ("xo", 4), ("ye", 0), ("ye", 1), ("ye", 7), ("ye", 2), ("ye", 6), ("ye", 3), ("ye", 5),
    ("ye", 4), ("mm", 4), ("bkh", 1), ("xo", 5), ("xe", 3), ("xr", 4), ("mm", 5, 0), ("xr", 5), ("mm", 5, 1),
    ("xf", 4), ("xf", 5), ("xe", 4), ("mm", 6, 0), ("xe", 5), ("mm", 6, 1),
)


UNITS = (
    ((0, 1), (0,)),
    ((0, 1), (1,)),
    ((0, 1), (3,)),
    ((2,), (0, 1, 3)),
    ((0, 1, 2), (2,)),
    ((3,), (0, 1, 2, 3)),
    ((4,), (0, 1, 2, 3)),
)


def wait_on(ref, sem):
    pltpu.make_async_copy(ref, ref, sem).wait()


def remote(src, dst, send_sem, recv_sem, device):
    return pltpu.make_async_remote_copy(
        src_ref=src,
        dst_ref=dst,
        send_sem=send_sem,
        recv_sem=recv_sem,
        device_id=device,
        device_id_type=MESH,
    )


def partner(k, y, z):
    turn = (k * 11) % FRAMES
    return ((y + turn // NZ) % NY) * NZ + (z + turn % NZ) % NZ


class WeightRing:
    def __init__(self, rows, zs, zr, ys, yr, head, y, z):
        self.rows, self.zs, self.zr, self.ys, self.yr = rows, zs, zr, ys, yr
        self.z = z
        self.z_next = (y * NZ + (z + 1) % NZ, head)
        self.z_prev = (y * NZ + (z + NZ - 1) % NZ, head)
        self.y_next = (((y + 1) % NY) * NZ + z, head)
        self.y_prev = (((y + NY - 1) % NY) * NZ + z, head)

    def block(self, d, dz, half=None):
        unit = ((self.z + dz) % NZ) * 10
        if half is None:
            return self.rows[d].at[pl.ds(unit, 10)]
        return self.rows[d].at[pl.ds(unit + half * 5, 5)]

    def send_z(self, t):
        up = self.block(0, NZ + 1 - t, None if t < 4 else 0)
        down = self.block(0, t - 1, None if t < 4 else 1)
        remote(up, up, self.zs.at[0, t - 1], self.zr.at[0, t - 1], self.z_next).start()
        remote(down, down, self.zs.at[1, t - 1], self.zr.at[1, t - 1], self.z_prev).start()

    def wait_z(self, t):
        wait_on(self.block(0, NZ - t, None if t < 4 else 0), self.zr.at[0, t - 1])
        wait_on(self.block(0, t, None if t < 4 else 1), self.zr.at[1, t - 1])

    def send_y(self, dz):
        own = self.block(0, dz)
        remote(own, self.block(3, dz), self.ys.at[0, dz], self.yr.at[0, dz], self.y_next).start()
        remote(own, self.block(1, dz), self.ys.at[1, dz], self.yr.at[1, dz], self.y_prev).start()

    def relay_y(self, dz):
        for way, d, to in ((0, 3, self.y_next), (1, 1, self.y_prev)):
            wait_on(self.block(d, dz), self.yr.at[way, dz])
            remote(
                self.block(d, dz, way),
                self.block(2, dz, way),
                self.ys.at[2 + way, dz],
                self.yr.at[2 + way, dz],
                to,
            ).start()

    def finish_y(self, dz):
        for way in range(2):
            wait_on(self.block(2, dz, way), self.yr.at[2 + way, dz])

    def drain(self):
        whole, half = self.block(0, 0), self.block(0, 0, 0)
        for t in range(1, 5):
            for way in range(2):
                wait_on(whole if t < 4 else half, self.zs.at[way, t - 1])
        for dz in range(NZ):
            for way in range(4):
                wait_on(whole if way < 2 else half, self.ys.at[way, dz])


class AttendedRing:
    def __init__(self, groups, send, recv, frame, x, core):
        self.groups, self.send, self.recv = groups, send, recv
        self.x, self.core = x, core
        self.next = (frame, ((x + 1) % NX) * 2 + core)
        self.prev = (frame, ((x + NX - 1) % NX) * 2 + core)
        self.other = (frame, x * 2 + 1 - core)

    def whole(self, x, core):
        return self.groups.at[(x % NX) * 2 + core]

    def half(self, x, core, k):
        return self.groups.at[(x % NX) * 2 + core, pl.ds(k * (FRAMES // 2), FRAMES // 2)]

    def copy(self, ref, k, device):
        remote(ref, ref, self.send.at[k], self.recv.at[k], device).start()

    def own(self):
        mine = self.whole(self.x, self.core)
        self.copy(mine, 0, self.next)
        self.copy(mine, 1, self.prev)
        self.copy(mine, 2, self.other)

    def relay(self):
        came = self.whole(self.x + NX - 1, self.core)
        wait_on(came, self.recv.at[0])
        self.copy(self.half(self.x + NX - 1, self.core, 0), 3, self.next)
        self.copy(came, 5, self.other)
        came = self.whole(self.x + 1, self.core)
        wait_on(came, self.recv.at[1])
        self.copy(self.half(self.x + 1, self.core, 1), 4, self.prev)
        self.copy(came, 6, self.other)

    def relay_far(self):
        for k in range(2):
            came = self.half(self.x + 2, self.core, k)
            wait_on(came, self.recv.at[3 + k])
            self.copy(came, 7 + k, self.other)

    def finish(self):
        across = 1 - self.core
        wait_on(self.whole(self.x, across), self.recv.at[2])
        wait_on(self.whole(self.x + NX - 1, across), self.recv.at[5])
        wait_on(self.whole(self.x + 1, across), self.recv.at[6])
        wait_on(self.half(self.x + 2, across, 0), self.recv.at[7])
        wait_on(self.half(self.x + 2, across, 1), self.recv.at[8])

    def drain(self):
        whole, half = self.whole(self.x, self.core), self.half(self.x, self.core, 0)
        for k in (0, 1, 2, 5, 6):
            wait_on(whole, self.send.at[k])
        for k in (3, 4, 7, 8):
            wait_on(half, self.send.at[k])


def softmax_rows(scores):
    largest = jnp.max(scores, axis=-1, keepdims=True)
    expo = jnp.exp2((scores - largest) * EXP_SCALE)
    return expo.astype(BF16), jnp.sum(expo, axis=-1, keepdims=True)


def dot_t(a, b):
    return lax.dot_general(a, b, (((1,), (1,)), ((), ())), preferred_element_type=F32)


def block_kernel(
    labels,
    q_hbm,
    k_hbm,
    v_hbm,
    w_hbm,
    out,
    table,
    heads_in,
    slots,
    got,
    mixed,
    either_spatial,
    either_temporal,
    gathered,
    weight0,
    weight1,
    weight2,
    weight3,
    picked_weight,
    total,
    result,
    load_sem,
    out_sem,
    fwd_send,
    fwd_recv,
    ret_send,
    ret_recv,
    wz_send,
    wz_recv,
    wy_send,
    wy_recv,
    x_send,
    x_recv,
):
    frame, head = lax.axis_index("frame"), lax.axis_index("head")
    y, z = frame // NZ, frame % NZ
    weight = (weight0, weight1, weight2, weight3)
    x, core = head // 2, head % 2

    loads = [
        pltpu.make_async_copy(
            w_hbm.at[pl.ds(n * 16, 16), :], weight0.at[z * 10 + n], load_sem.at[3, n]
        )
        for n in range(10)
    ]
    loads += [
        pltpu.make_async_copy(
            source.at[:, pl.ds(h * HDIM, HDIM)], heads_in.at[n, h], load_sem.at[n, h]
        )
        for n, source in enumerate((q_hbm, k_hbm, v_hbm))
        for h in range(HEAD_DEV)
    ]
    for load in loads:
        load.start()

    barrier = pltpu.get_barrier_semaphore()

    def greet(k, carry):
        pl.semaphore_signal(
            barrier, inc=1, device_id=((frame + k) % FRAMES, head), device_id_type=MESH
        )
        return carry

    lax.fori_loop(1, FRAMES, greet, 0)
    for there in (((x + 1) % NX) * 2 + core, ((x + NX - 1) % NX) * 2 + core, x * 2 + 1 - core):
        pl.semaphore_signal(barrier, inc=1, device_id=(frame, there), device_id_type=MESH)

    def fill(g, line):
        label = [labels[g * HEAD_DEV + h] for h in range(HEAD_DEV)]
        temporal_count = sum(label)
        rank, ones = [], 0
        for h in range(HEAD_DEV):
            rank.append(label[h] * (HEAD_DEV - temporal_count + ones) + (1 - label[h]) * (h - ones))
            ones = ones + label[h]
        for slot in range(HEAD_DEV):
            table[line * 8 + slot] = sum(
                h * (rank[h] == slot).astype(jnp.int32) for h in range(HEAD_DEV)
            )
        table[line * 8 + HEAD_DEV] = temporal_count - 2

    fill(head, 0)
    for g in range(GROUPS):
        fill(g, 1 + g)

    def pick(slot):
        if slot == SLOT_EITHER:
            for load in loads[10:]:
                load.wait()
        for n in range(3):
            slots[slot, n] = heads_in[n, table[slot]].reshape(TILED)

    for load in loads[:10]:
        load.wait()
    pl.semaphore_wait(barrier, FRAMES - 1 + 3)

    ring = WeightRing(weight, wz_send, wz_recv, wy_send, wy_recv, head, y, z)
    gather = [
        AttendedRing(ref, x_send.at[n], x_recv.at[n], frame, x, core)
        for n, ref in enumerate(
            [gathered.at[slot] for slot in range(4)] + [gathered.at[4, :, :, h] for h in range(2)]
        )
    ]

    def send_forward(sem, first, last, source, target):
        def one(k, carry):
            to = partner(k, y, z)
            remote(
                source(to), target(frame), fwd_send.at[sem], fwd_recv.at[sem], (to, head)
            ).start()
            return carry

        lax.fori_loop(first, last, one, 0)
        if first == 1:
            pltpu.make_async_copy(source(frame), target(frame), fwd_recv.at[sem]).start()

    def forward(s, part):
        send_forward(
            s,
            max(1, part * 8),
            part * 8 + 8,
            lambda to: slots.at[SENT[s], :, to],
            lambda here: got.at[s, :, here],
        )

    def forward_half(h, part):
        send_forward(
            2 + h,
            max(1, part * 16),
            part * 16 + 16,
            lambda to: slots.at[4, :, to, h],
            lambda here: got.at[2, :, here, h],
        )

    def returned(s):
        return either_temporal if SENT[s] == SLOT_EITHER else gathered.at[SENT[s], head]

    def send_back(sem, source, target):
        def one(k, carry):
            to = partner(k, y, z)
            remote(
                source(to), target(frame), ret_send.at[sem], ret_recv.at[sem], (to, head)
            ).start()
            return carry

        lax.fori_loop(1, FRAMES, one, 0)
        pltpu.make_async_copy(source(frame), target(frame), ret_recv.at[sem]).start()

    def spatial(slot):
        def one(i, carry):
            blocks = pl.ds(i * 8, 8)
            query = slots[slot, 0, blocks].reshape(256, HDIM)
            key, value = (slots[slot, n].reshape(POS, HDIM) for n in (1, 2))
            expo, row_sum = softmax_rows(dot_t(query, key))
            mix = jnp.dot(expo, value, preferred_element_type=F32)
            mix = (mix / row_sum).astype(BF16).reshape(8, 2, HALF, HDIM)
            if slot == SLOT_EITHER:
                either_spatial[blocks] = mix
            else:
                gathered[slot, head, blocks] = mix
            return carry

        lax.fori_loop(0, POS // 256, one, 0)

    def temporal(s, h):
        rows = FRAMES * HALF
        row_at = lax.broadcasted_iota(jnp.int32, (rows, rows), 0) % HALF
        col_at = lax.broadcasted_iota(jnp.int32, (rows, rows), 1) % HALF
        query, key, value = (got[s, n, :, h].reshape(rows, HDIM) for n in range(3))
        expo, row_sum = softmax_rows(jnp.where(row_at == col_at, dot_t(query, key), NEG))
        mix = jnp.dot(expo, value, preferred_element_type=F32)
        mixed[s, :, h] = (mix / row_sum).astype(BF16).reshape(FRAMES, HALF, HDIM)

    def attend_temporal(s):
        wait_on(got.at[s], fwd_recv.at[s])
        for h in range(2):
            temporal(s, h)
        send_back(s, lambda to: mixed.at[s, to], lambda here: returned(s).at[here])

    def attend_temporal_half(h):
        wait_on(got.at[2, :, :, h], fwd_recv.at[2 + h])
        temporal(2, h)
        send_back(
            2 + h, lambda to: mixed.at[2, to, h], lambda here: gathered.at[4, head, here, h]
        )

    def come_back(s):
        wait_on(returned(s), ret_recv.at[s])
        if SENT[s] == SLOT_EITHER:
            is_temporal = jnp.full(TILED, table[HEAD_DEV], jnp.int32) == 1
            gathered[SLOT_EITHER, head] = jnp.where(
                is_temporal, either_temporal[...], either_spatial[...]
            )

    def come_back_half(h):
        wait_on(gathered.at[4, head, :, h], ret_recv.at[2 + h])

    def groups_at(d):
        there = (y + d) % NY
        return [(there * 2 + c, c) for c in range(2)]

    def pick_weight(picks):
        for n, (slot, d, g, c) in enumerate(picks):
            at = (table[(1 + g) * 8 + slot] + c * HEAD_DEV) * 8
            for m in range(8):
                picked_weight[pl.ds(n * HDIM + m * 16, 16), :] = weight[d][at + m]

    def project(unit, part=None):
        taken, offsets = UNITS[unit]
        picks = [(slot, d, g, c) for slot in taken for d in offsets for g, c in groups_at(d)]
        depth = len(picks) * HDIM
        if part != 1:
            pick_weight(picks)

        def one(i, carry):
            at = (pl.ds(i * 8, 8),) if part is None else (pl.ds(i * 16, 16), part)
            left = jnp.concatenate(
                [gathered[(slot, g) + at].reshape(256, HDIM) for slot, d, g, c in picks], axis=1
            )
            sums = jnp.dot(left, picked_weight[:depth, :], preferred_element_type=F32)
            sums = sums.reshape(total[at].shape)
            if unit != 0:
                sums = sums + total[at]
            if taken == (4,):
                result[at] = sums.astype(BF16)
            else:
                total[at] = sums
            return carry

        lax.fori_loop(0, 4 if part is None else 2, one, 0)
        if taken == (4,):
            store(part).start()

    def store(h):
        return pltpu.make_async_copy(result.at[:, h], out.at[:, h], out_sem.at[h])

    acts = {
        "pick": pick,
        "zs": ring.send_z,
        "zw": ring.wait_z,
        "ys": ring.send_y,
        "yr": ring.relay_y,
        "ye": ring.finish_y,
        "fwd": forward,
        "fwh": forward_half,
        "sp": spatial,
        "tm": attend_temporal,
        "tmh": attend_temporal_half,
        "back": come_back,
        "bkh": come_back_half,
        "xo": lambda n: gather[n].own(),
        "xr": lambda n: gather[n].relay(),
        "xf": lambda n: gather[n].relay_far(),
        "xe": lambda n: gather[n].finish(),
        "mm": project,
    }
    for act, *at in ORDER:
        acts[act](*at)

    for h in range(2):
        store(h).wait()
    ring.drain()
    for each in gather:
        each.drain()
    for s in range(2):
        wait_on(slots.at[SENT[s], :, pl.ds(0, FRAMES - 1)], fwd_send.at[s])
        wait_on(mixed.at[s, pl.ds(0, FRAMES - 1)], ret_send.at[s])
    for h in range(2):
        wait_on(slots.at[4, :, pl.ds(0, FRAMES - 1), h], fwd_send.at[2 + h])
        wait_on(mixed.at[2, pl.ds(0, FRAMES - 1), h], ret_send.at[2 + h])


def per_device(queries, key_states, value_states, out_weight, head_labels):
    any_spec = pl.BlockSpec(memory_space=pl.ANY)
    dma = pltpu.SemaphoreType.DMA
    return pl.pallas_call(
        block_kernel,
        out_shape=pltpu.VMEM((FRAMES, 2, HALF, COLS), BF16),
        in_specs=[pl.BlockSpec(memory_space=pltpu.SMEM)] + [any_spec] * 4,
        out_specs=any_spec,
        scratch_shapes=[
            pltpu.SMEM(((1 + GROUPS) * 8,), jnp.int32),
            pltpu.VMEM((3, HEAD_DEV, POS, HDIM), BF16),
            pltpu.VMEM((HEAD_DEV, 3) + TILED, BF16),
            pltpu.VMEM((3, 3) + TILED, BF16),
            pltpu.VMEM((3,) + TILED, BF16),
            pltpu.VMEM(TILED, BF16),
            pltpu.VMEM(TILED, BF16),
            pltpu.VMEM((HEAD_DEV, GROUPS) + TILED, BF16),
            pltpu.VMEM((WROWS * NZ // 16, 16, COLS), BF16),
            pltpu.VMEM((WROWS * NZ // 16, 16, COLS), BF16),
            pltpu.VMEM((WROWS * NZ // 16, 16, COLS), BF16),
            pltpu.VMEM((WROWS * NZ // 16, 16, COLS), BF16),
            pltpu.VMEM((GROUPS * HDIM, COLS), BF16),
            pltpu.VMEM((FRAMES, 2, HALF, COLS), F32),
            pltpu.VMEM((FRAMES, 2, HALF, COLS), BF16),
            dma((4, 10)),
            dma((2,)),
            dma((4,)),
            dma((4,)),
            dma((4,)),
            dma((4,)),
            dma((2, 4)),
            dma((2, 4)),
            dma((4, NZ)),
            dma((4, NZ)),
            dma((HEAD_DEV + 1, 9)),
            dma((HEAD_DEV + 1, 9)),
        ],
        compiler_params=pltpu.CompilerParams(
            collective_id=0, has_side_effects=True, vmem_limit_bytes=56 << 20
        ),
        name="block_kernel",
    )(head_labels, queries, key_states, value_states, out_weight).reshape(POS, COLS)


def solution(mesh):
    return jax.shard_map(
        per_device,
        mesh=mesh,
        in_specs=(
            P("frame", "head"),
            P("frame", "head"),
            P("frame", "head"),
            P("frame", "head"),
            P(),
        ),
        out_specs=P("frame", "head"),
        check_vma=False,
    )
```

```python
import functools
import math

import jax
import jax.numpy as jnp
from jax import lax
from jax.experimental import pallas as pl
from jax.experimental.pallas import tpu as pltpu
from jax.sharding import PartitionSpec as P

MESH = pl.DeviceIdType.MESH
BF16 = jnp.bfloat16
F32 = jnp.float32
HDIM = 128
POS = 1024
FRAMES = 32
NY, NZ, NX = 4, 8, 4
GROUPS = 8
HEAD_DEV = 5
PB = POS // FRAMES
WROWS = 160
COLS = 640
EXP_SCALE = HDIM**-0.5 * math.log2(math.e)
NEG = -1e30
HALF = PB // 2
TILED = (FRAMES, 2, HALF, HDIM)

SLOT_EITHER = 2
SENT = (2, 3, 4)

ORDER = (
    ("zs", 1), ("ys", 0), ("pick", 2), ("fwd", 0, 0), ("fwd", 0, 1), ("pick", 0), ("pick", 1), ("pick", 3),
    ("pick", 4), ("fill",), ("zw", 1), ("zs", 2), ("ys", 1), ("ys", 7), ("fwd", 0, 2), ("fwd", 0, 3),
    ("sp", 0), ("xo", 0), ("yw", 0), ("yr", 0), ("zw", 2), ("ys", 2), ("ys", 6), ("fwd", 1, 0), ("fwd", 1, 1),
    ("zs", 3), ("fwd", 1, 2), ("fwd", 1, 3), ("sp", 1), ("xo", 1), ("yw", 1), ("yr", 1), ("yw", 7), ("yr", 7),
    ("tm", 0), ("sp", 2), ("xr", 0), ("xf", 0), ("yw", 2), ("yr", 2), ("yw", 6), ("yr", 6), ("zw", 3),
    ("zs", 4), ("ys", 3), ("ys", 5), ("fwh", 0, 0), ("xr", 1), ("xf", 1), ("back", 0), ("xo", 2), ("tm", 1),
    ("fwh", 0, 1), ("fwh", 1, 0), ("zw", 4), ("ys", 4), ("fwh", 1, 1), ("xe", 0), ("xe", 1), ("mm", 0),
    ("yw", 3), ("yr", 3), ("xr", 2), ("yw", 5), ("yr", 5), ("xf", 2), ("xe", 2), ("tmh", 0), ("back", 1),
    ("xo", 3), ("yw", 4), ("yr", 4), ("mm", 1), ("tmh", 1), ("xr", 3), ("mm", 2), ("bkh", 0), ("xo", 4),
    ("mm", 3), ("xf", 3), ("ye",), ("mm", 4), ("bkh", 1), ("xo", 5), ("xr", 4), ("xe", 3), ("mm", 5, 0),
    ("mm", 5, 1), ("xr", 5), ("xf", 4), ("xe", 4), ("mm", 6, 0), ("xf", 5), ("xe", 5), ("mm", 6, 1),
)


UNITS = (
    ((0, 1), (0,)),
    ((0, 1), (1,)),
    ((0, 1), (3,)),
    ((2,), (0, 1, 3)),
    ((0, 1, 2), (2,)),
    ((3,), (0, 1, 2, 3)),
    ((4,), (0, 1, 2, 3)),
)


def wait_on(ref, sem):
    pltpu.make_async_copy(ref, ref, sem).wait()


def remote(src, dst, send_sem, recv_sem, device):
    return pltpu.make_async_remote_copy(
        src_ref=src,
        dst_ref=dst,
        send_sem=send_sem,
        recv_sem=recv_sem,
        device_id=device,
        device_id_type=MESH,
    )


def partner(k, y, z):
    turn = (k * 11) % FRAMES
    return ((y + turn // NZ) % NY) * NZ + (z + turn % NZ) % NZ


class WeightRing:
    def __init__(self, rows, zs, zr, ys, yr, far, head, y, z):
        self.rows, self.zs, self.zr, self.ys, self.yr, self.far = rows, zs, zr, ys, yr, far
        self.z = z
        self.z_next = (y * NZ + (z + 1) % NZ, head)
        self.z_prev = (y * NZ + (z + NZ - 1) % NZ, head)
        self.y_next = (((y + 1) % NY) * NZ + z, head)
        self.y_prev = (((y + NY - 1) % NY) * NZ + z, head)

    def block(self, d, dz, half=None):
        unit = ((self.z + dz) % NZ) * 10
        if half is None:
            return self.rows[d].at[pl.ds(unit, 10)]
        return self.rows[d].at[pl.ds(unit + half * 5, 5)]

    def send_z(self, t):
        up = self.block(0, NZ + 1 - t, None if t < 4 else 0)
        down = self.block(0, t - 1, None if t < 4 else 1)
        remote(up, up, self.zs.at[0], self.zr.at[0, t - 1], self.z_next).start()
        remote(down, down, self.zs.at[1], self.zr.at[1, t - 1], self.z_prev).start()

    def wait_z(self, t):
        wait_on(self.block(0, NZ - t, None if t < 4 else 0), self.zr.at[0, t - 1])
        wait_on(self.block(0, t, None if t < 4 else 1), self.zr.at[1, t - 1])

    def send_y(self, dz):
        own = self.block(0, dz)
        remote(own, self.block(3, dz), self.ys.at[0], self.yr.at[0, dz], self.y_next).start()
        remote(own, self.block(1, dz), self.ys.at[1], self.yr.at[1, dz], self.y_prev).start()

    def wait_y(self, dz):
        wait_on(self.block(3, dz), self.yr.at[0, dz])
        wait_on(self.block(1, dz), self.yr.at[1, dz])

    def relay_y(self, dz):
        for way, d, to in ((0, 3, self.y_next), (1, 1, self.y_prev)):
            remote(
                self.block(d, dz, way),
                self.block(2, dz, way),
                self.ys.at[2 + way],
                self.far,
                to,
            ).start()

    def finish_y(self):
        wait_on(self.rows[2], self.far)

    def drain(self):
        for way in range(2):
            wait_on(self.rows[0].at[pl.ds(0, 35)], self.zs.at[way])
            wait_on(self.rows[0], self.ys.at[way])
            wait_on(self.rows[0].at[pl.ds(0, 40)], self.ys.at[2 + way])


class AttendedRing:
    def __init__(self, groups, send, recv, frame, x, core):
        self.groups, self.send, self.recv = groups, send, recv
        self.x, self.core = x, core
        self.next = (frame, ((x + 1) % NX) * 2 + core)
        self.prev = (frame, ((x + NX - 1) % NX) * 2 + core)
        self.other = (frame, x * 2 + 1 - core)

    def whole(self, x, core):
        return self.groups.at[(x % NX) * 2 + core]

    def half(self, x, core, k):
        return self.groups.at[(x % NX) * 2 + core, pl.ds(k * (FRAMES // 2), FRAMES // 2)]

    def copy(self, ref, k, device):
        remote(ref, ref, self.send, self.recv.at[k], device).start()

    def own(self):
        mine = self.whole(self.x, self.core)
        self.copy(mine, 0, self.next)
        self.copy(mine, 1, self.prev)
        self.copy(mine, 4, self.other)

    def relay(self):
        for way, dx, to in ((0, NX - 1, self.next), (1, 1, self.prev)):
            came = self.whole(self.x + dx, self.core)
            wait_on(came, self.recv.at[way])
            self.copy(self.half(self.x + dx, self.core, way), 2 + way, to)
            self.copy(came, 4, self.other)

    def relay_far(self):
        for way in range(2):
            came = self.half(self.x + 2, self.core, way)
            wait_on(came, self.recv.at[2 + way])
            self.copy(came, 4, self.other)

    def finish(self):
        wait_on(self.groups.at[pl.ds(0, 4)], self.recv.at[4])

    def drain(self):
        wait_on(self.groups.at[pl.ds(0, 7)], self.send)


def softmax_rows(scores):
    largest = jnp.max(scores, axis=-1, keepdims=True)
    expo = jnp.exp2((scores - largest) * EXP_SCALE)
    return expo.astype(BF16), jnp.sum(expo, axis=-1, keepdims=True)


def dot_t(a, b):
    return lax.dot_general(a, b, (((1,), (1,)), ((), ())), preferred_element_type=F32)


def block_kernel(
    labels,
    q_hbm,
    k_hbm,
    v_hbm,
    w_hbm,
    out,
    table,
    heads_in,
    slots,
    got,
    mixed,
    either_spatial,
    either_temporal,
    gathered,
    weight0,
    weight1,
    weight2,
    weight3,
    picked_weight,
    total,
    result,
    load_sem,
    out_sem,
    fwd_send,
    fwd_recv,
    ret_send,
    ret_recv,
    wz_send,
    wz_recv,
    wy_send,
    wy_recv,
    far_recv,
    x_send,
    x_recv,
):
    frame, head = lax.axis_index("frame"), lax.axis_index("head")
    y, z = frame // NZ, frame % NZ
    weight = (weight0, weight1, weight2, weight3)
    x, core = head // 2, head % 2

    load_weight = pltpu.make_async_copy(w_hbm, weight0.at[pl.ds(z * 10, 10)], load_sem.at[0])
    load_weight.start()
    for n, source in enumerate((q_hbm, k_hbm, v_hbm)):
        for h in range(HEAD_DEV):
            pltpu.make_async_copy(
                source.at[:, pl.ds(h * HDIM, HDIM)], heads_in.at[n, h], load_sem.at[1]
            ).start()

    barrier = pltpu.get_barrier_semaphore()

    def greet(k, carry):
        pl.semaphore_signal(
            barrier, inc=1, device_id=((frame + k) % FRAMES, head), device_id_type=MESH
        )
        return carry

    lax.fori_loop(1, FRAMES, greet, 0)
    for there in (((x + 1) % NX) * 2 + core, ((x + NX - 1) % NX) * 2 + core, x * 2 + 1 - core):
        pl.semaphore_signal(barrier, inc=1, device_id=(frame, there), device_id_type=MESH)

    def fill(g, line):
        label = [labels[g * HEAD_DEV + h] for h in range(HEAD_DEV)]
        temporal_count = sum(label)
        rank, ones = [], 0
        for h in range(HEAD_DEV):
            rank.append(label[h] * (HEAD_DEV - temporal_count + ones) + (1 - label[h]) * (h - ones))
            ones = ones + label[h]
        for slot in range(HEAD_DEV):
            table[line * 8 + slot] = sum(
                h * (rank[h] == slot).astype(jnp.int32) for h in range(HEAD_DEV)
            )
        table[line * 8 + HEAD_DEV] = temporal_count - 2

    def fill_all():
        for g in range(GROUPS):
            fill(g, 1 + g)

    def pick(slot):
        if slot == SLOT_EITHER:
            wait_on(heads_in, load_sem.at[1])
        for n in range(3):
            slots[slot, n] = heads_in[n, table[slot]].reshape(TILED)

    fill(head, 0)
    load_weight.wait()
    pl.semaphore_wait(barrier, FRAMES - 1 + 3)

    ring = WeightRing(weight, wz_send, wz_recv, wy_send, wy_recv, far_recv.at[0], head, y, z)
    gather = [
        AttendedRing(ref, x_send.at[n], x_recv.at[n], frame, x, core)
        for n, ref in enumerate(
            [gathered.at[slot] for slot in range(4)] + [gathered.at[4, :, :, h] for h in range(2)]
        )
    ]

    def send_forward(sem, first, last, source, target):
        def one(k, carry):
            to = partner(k, y, z)
            remote(
                source(to), target(frame), fwd_send.at[sem], fwd_recv.at[sem], (to, head)
            ).start()
            return carry

        lax.fori_loop(first, last, one, 0)
        if first == 1:
            pltpu.make_async_copy(source(frame), target(frame), fwd_recv.at[sem]).start()

    def forward(s, part):
        send_forward(
            s,
            max(1, part * 8),
            part * 8 + 8,
            lambda to: slots.at[SENT[s], :, to],
            lambda here: got.at[s, :, here],
        )

    def forward_half(h, part):
        send_forward(
            2 + h,
            max(1, part * 16),
            part * 16 + 16,
            lambda to: slots.at[4, :, to, h],
            lambda here: got.at[2, :, here, h],
        )

    def returned(s):
        return either_temporal if SENT[s] == SLOT_EITHER else gathered.at[SENT[s], head]

    def send_back(sem, source, target):
        def one(k, carry):
            to = partner(k, y, z)
            remote(
                source(to), target(frame), ret_send.at[sem], ret_recv.at[sem], (to, head)
            ).start()
            return carry

        lax.fori_loop(1, FRAMES, one, 0)
        pltpu.make_async_copy(source(frame), target(frame), ret_recv.at[sem]).start()

    def spatial(slot):
        def one(i, carry):
            blocks = pl.ds(i * 8, 8)
            query = slots[slot, 0, blocks].reshape(256, HDIM)
            key, value = (slots[slot, n].reshape(POS, HDIM) for n in (1, 2))
            expo, row_sum = softmax_rows(dot_t(query, key))
            mix = jnp.dot(expo, value, preferred_element_type=F32)
            mix = (mix / row_sum).astype(BF16).reshape(8, 2, HALF, HDIM)
            if slot == SLOT_EITHER:
                either_spatial[blocks] = mix
            else:
                gathered[slot, head, blocks] = mix
            return carry

        lax.fori_loop(0, POS // 256, one, 0)

    def temporal(s, h):
        rows = FRAMES * HALF
        row_at = lax.broadcasted_iota(jnp.int32, (rows, rows), 0) % HALF
        col_at = lax.broadcasted_iota(jnp.int32, (rows, rows), 1) % HALF
        query, key, value = (got[s, n, :, h].reshape(rows, HDIM) for n in range(3))
        expo, row_sum = softmax_rows(jnp.where(row_at == col_at, dot_t(query, key), NEG))
        mix = jnp.dot(expo, value, preferred_element_type=F32)
        mixed[s, :, h] = (mix / row_sum).astype(BF16).reshape(FRAMES, HALF, HDIM)

    def attend_temporal(s):
        wait_on(got.at[s], fwd_recv.at[s])
        for h in range(2):
            temporal(s, h)
        send_back(s, lambda to: mixed.at[s, to], lambda here: returned(s).at[here])

    def attend_temporal_half(h):
        wait_on(got.at[2, :, :, h], fwd_recv.at[2 + h])
        temporal(2, h)
        send_back(
            2 + h, lambda to: mixed.at[2, to, h], lambda here: gathered.at[4, head, here, h]
        )

    def come_back(s):
        wait_on(returned(s), ret_recv.at[s])
        if SENT[s] == SLOT_EITHER:
            is_temporal = jnp.full(TILED, table[HEAD_DEV], jnp.int32) == 1
            gathered[SLOT_EITHER, head] = jnp.where(
                is_temporal, either_temporal[...], either_spatial[...]
            )

    def come_back_half(h):
        wait_on(gathered.at[4, head, :, h], ret_recv.at[2 + h])

    def groups_at(d):
        there = (y + d) % NY
        return [(there * 2 + c, c) for c in range(2)]

    def pick_weight(picks):
        for n, (slot, d, g, c) in enumerate(picks):
            at = (table[(1 + g) * 8 + slot] + c * HEAD_DEV) * 8
            for m in range(8):
                picked_weight[pl.ds(n * HDIM + m * 16, 16), :] = weight[d][at + m]

    def project(unit, part=None):
        taken, offsets = UNITS[unit]
        picks = [(slot, d, g, c) for slot in taken for d in offsets for g, c in groups_at(d)]
        depth = len(picks) * HDIM
        if part != 1:
            pick_weight(picks)

        def one(i, carry):
            at = (pl.ds(i * 8, 8),) if part is None else (pl.ds(i * 16, 16), part)
            left = jnp.concatenate(
                [gathered[(slot, g) + at].reshape(256, HDIM) for slot, d, g, c in picks], axis=1
            )
            sums = jnp.dot(left, picked_weight[:depth, :], preferred_element_type=F32)
            sums = sums.reshape(total[at].shape)
            if unit != 0:
                sums = sums + total[at]
            if taken == (4,):
                result[at] = sums.astype(BF16)
            else:
                total[at] = sums
            return carry

        lax.fori_loop(0, 4 if part is None else 2, one, 0)
        if taken == (4,):
            store(part).start()

    def store(h):
        return pltpu.make_async_copy(result.at[:, h], out.at[:, h], out_sem.at[h])

    acts = {
        "pick": pick,
        "fill": fill_all,
        "zs": ring.send_z,
        "zw": ring.wait_z,
        "ys": ring.send_y,
        "yw": ring.wait_y,
        "yr": ring.relay_y,
        "ye": ring.finish_y,
        "fwd": forward,
        "fwh": forward_half,
        "sp": spatial,
        "tm": attend_temporal,
        "tmh": attend_temporal_half,
        "back": come_back,
        "bkh": come_back_half,
        "xo": lambda n: gather[n].own(),
        "xr": lambda n: gather[n].relay(),
        "xf": lambda n: gather[n].relay_far(),
        "xe": lambda n: gather[n].finish(),
        "mm": project,
    }
    for act, *at in ORDER:
        acts[act](*at)

    for h in range(2):
        store(h).wait()
    ring.drain()
    for each in gather:
        each.drain()
    for s in range(2):
        wait_on(slots.at[SENT[s], :, pl.ds(0, FRAMES - 1)], fwd_send.at[s])
        wait_on(mixed.at[s, pl.ds(0, FRAMES - 1)], ret_send.at[s])
    for h in range(2):
        wait_on(slots.at[4, :, pl.ds(0, FRAMES - 1), h], fwd_send.at[2 + h])
        wait_on(mixed.at[2, pl.ds(0, FRAMES - 1), h], ret_send.at[2 + h])


def per_device(queries, key_states, value_states, out_weight, head_labels):
    any_spec = pl.BlockSpec(memory_space=pl.ANY)
    dma = pltpu.SemaphoreType.DMA
    return pl.pallas_call(
        block_kernel,
        out_shape=pltpu.VMEM((FRAMES, 2, HALF, COLS), BF16),
        in_specs=[pl.BlockSpec(memory_space=pltpu.SMEM)] + [any_spec] * 4,
        out_specs=any_spec,
        scratch_shapes=[
            pltpu.SMEM(((1 + GROUPS) * 8,), jnp.int32),
            pltpu.VMEM((3, HEAD_DEV, POS, HDIM), BF16),
            pltpu.VMEM((HEAD_DEV, 3) + TILED, BF16),
            pltpu.VMEM((3, 3) + TILED, BF16),
            pltpu.VMEM((3,) + TILED, BF16),
            pltpu.VMEM(TILED, BF16),
            pltpu.VMEM(TILED, BF16),
            pltpu.VMEM((HEAD_DEV, GROUPS) + TILED, BF16),
            pltpu.VMEM((WROWS * NZ // 16, 16, COLS), BF16),
            pltpu.VMEM((WROWS * NZ // 16, 16, COLS), BF16),
            pltpu.VMEM((WROWS * NZ // 16, 16, COLS), BF16),
            pltpu.VMEM((WROWS * NZ // 16, 16, COLS), BF16),
            pltpu.VMEM((GROUPS * HDIM, COLS), BF16),
            pltpu.VMEM((FRAMES, 2, HALF, COLS), F32),
            pltpu.VMEM((FRAMES, 2, HALF, COLS), BF16),
            dma((2,)),
            dma((2,)),
            dma((4,)),
            dma((4,)),
            dma((4,)),
            dma((4,)),
            dma((2,)),
            dma((2, 4)),
            dma((4,)),
            dma((2, NZ)),
            dma((1,)),
            dma((HEAD_DEV + 1,)),
            dma((HEAD_DEV + 1, 5)),
        ],
        compiler_params=pltpu.CompilerParams(
            collective_id=0, has_side_effects=True, vmem_limit_bytes=56 << 20
        ),
        name="block_kernel",
    )(head_labels, queries, key_states, value_states, out_weight.reshape(10, 16, COLS)).reshape(POS, COLS)


def solution(mesh):
    return jax.shard_map(
        per_device,
        mesh=mesh,
        in_specs=(
            P("frame", "head"),
            P("frame", "head"),
            P("frame", "head"),
            P("frame", "head"),
            P(),
        ),
        out_specs=P("frame", "head"),
        check_vma=False,
    )
```

```python
import functools
import math

import jax
import jax.numpy as jnp
from jax import lax
from jax.experimental import pallas as pl
from jax.experimental.pallas import tpu as pltpu
from jax.sharding import PartitionSpec as P

MESH = pl.DeviceIdType.MESH
BF16 = jnp.bfloat16
F32 = jnp.float32
HDIM = 128
POS = 1024
FRAMES = 32
NY, NZ, NX = 4, 8, 4
GROUPS = 8
HEAD_DEV = 5
PB = POS // FRAMES
WROWS = 160
COLS = 640
EXP_SCALE = HDIM**-0.5 * math.log2(math.e)
NEG = -1e30
SPLIT_FROM = 4
HALF = PB // 2
TILED = (FRAMES, 2, HALF, HDIM)

SLOT_EITHER = 2
SENT = (2, 3, 4)

ORDER = (
    ("zs", 1), ("ys", 0), ("pick", 2), ("fwd", 0, 0), ("fwd", 0, 1), ("pick", 0), ("pick", 1), ("pick", 3),
    ("pick", 4), ("fill",), ("zw", 1), ("zs", 2), ("ys", 1), ("ys", 7), ("fwd", 0, 2), ("fwd", 0, 3),
    ("sp", 0), ("xo", 0), ("yw", 0), ("yr", 0), ("zw", 2), ("ys", 2), ("ys", 6), ("fwd", 1, 0), ("fwd", 1, 1),
    ("zs", 3), ("fwd", 1, 2), ("fwd", 1, 3), ("sp", 1), ("xo", 1), ("yw", 1), ("yr", 1), ("yw", 7), ("yr", 7),
    ("tm", 0), ("sp", 2), ("xr", 0), ("xf", 0), ("yw", 2), ("yr", 2), ("yw", 6), ("yr", 6), ("zw", 3),
    ("zs", 4), ("ys", 3), ("ys", 5), ("fwh", 0, 0), ("xr", 1), ("xf", 1), ("back", 0), ("xo", 2), ("tm", 1),
    ("fwh", 0, 1), ("fwh", 1, 0), ("zw", 4), ("ys", 4), ("fwh", 1, 1), ("xe", 0), ("xe", 1), ("mm", 0),
    ("yw", 3), ("yr", 3), ("xr", 2), ("xf", 2), ("yw", 5), ("yr", 5), ("xe", 2), ("tmh", 0), ("back", 1),
    ("xo", 3), ("yw", 4), ("yr", 4), ("mm", 1), ("tmh", 1), ("xr", 3), ("mm", 2), ("bkh", 0), ("xo", 4),
    ("mm", 3), ("xf", 3), ("ye",), ("mm", 4), ("bkh", 1), ("xo", 5), ("xr", 4), ("xe", 3), ("mm", 5, 0),
    ("mm", 5, 1), ("xr", 5), ("xf", 4), ("xe", 4), ("mm", 6, 0), ("xf", 5), ("xe", 5), ("mm", 6, 1),
)


UNITS = (
    ((0, 1), (0,)),
    ((0, 1), (1,)),
    ((0, 1), (3,)),
    ((2,), (0, 1, 3)),
    ((0, 1, 2), (2,)),
    ((3,), (0, 1, 2, 3)),
    ((4,), (0, 1, 2, 3)),
)


def wait_on(ref, sem):
    pltpu.make_async_copy(ref, ref, sem).wait()


def remote(src, dst, send_sem, recv_sem, device):
    return pltpu.make_async_remote_copy(
        src_ref=src,
        dst_ref=dst,
        send_sem=send_sem,
        recv_sem=recv_sem,
        device_id=device,
        device_id_type=MESH,
    )


def partner(k, y, z):
    turn = (k * 11) % FRAMES
    return ((y + turn // NZ) % NY) * NZ + (z + turn % NZ) % NZ


class WeightRing:
    def __init__(self, rows, zs, zr, ys, yr, far, head, y, z):
        self.rows, self.zs, self.zr, self.ys, self.yr, self.far = rows, zs, zr, ys, yr, far
        self.z = z
        self.z_next = (y * NZ + (z + 1) % NZ, head)
        self.z_prev = (y * NZ + (z + NZ - 1) % NZ, head)
        self.y_next = (((y + 1) % NY) * NZ + z, head)
        self.y_prev = (((y + NY - 1) % NY) * NZ + z, head)

    def block(self, d, dz, half=None):
        unit = ((self.z + dz) % NZ) * 10
        if half is None:
            return self.rows[d].at[pl.ds(unit, 10)]
        return self.rows[d].at[pl.ds(unit + half * 5, 5)]

    def send_z(self, t):
        up = self.block(0, NZ + 1 - t, None if t < 4 else 0)
        down = self.block(0, t - 1, None if t < 4 else 1)
        remote(up, up, self.zs.at[0], self.zr.at[0, t - 1], self.z_next).start()
        remote(down, down, self.zs.at[1], self.zr.at[1, t - 1], self.z_prev).start()

    def wait_z(self, t):
        wait_on(self.block(0, NZ - t, None if t < 4 else 0), self.zr.at[0, t - 1])
        wait_on(self.block(0, t, None if t < 4 else 1), self.zr.at[1, t - 1])

    def send_y(self, dz):
        own = self.block(0, dz)
        remote(own, self.block(3, dz), self.ys.at[0], self.yr.at[0, dz], self.y_next).start()
        remote(own, self.block(1, dz), self.ys.at[1], self.yr.at[1, dz], self.y_prev).start()

    def wait_y(self, dz):
        wait_on(self.block(3, dz), self.yr.at[0, dz])
        wait_on(self.block(1, dz), self.yr.at[1, dz])

    def relay_y(self, dz):
        for way, d, to in ((0, 3, self.y_next), (1, 1, self.y_prev)):
            remote(
                self.block(d, dz, way),
                self.block(2, dz, way),
                self.ys.at[2 + way],
                self.far,
                to,
            ).start()

    def finish_y(self):
        wait_on(self.rows[2], self.far)

    def drain(self):
        for way in range(2):
            wait_on(self.rows[0].at[pl.ds(0, 35)], self.zs.at[way])
            wait_on(self.rows[0], self.ys.at[way])
            wait_on(self.rows[0].at[pl.ds(0, 40)], self.ys.at[2 + way])


class AttendedRing:
    def __init__(self, groups, send, recv, split, frame, x, core):
        self.groups, self.send, self.recv, self.split = groups, send, recv, split
        self.x, self.core = x, core
        self.next = (frame, ((x + 1) % NX) * 2 + core)
        self.prev = (frame, ((x + NX - 1) % NX) * 2 + core)
        self.other = (frame, x * 2 + 1 - core)

    def whole(self, x, core):
        return self.groups.at[(x % NX) * 2 + core]

    def half(self, x, core, k):
        return self.groups.at[(x % NX) * 2 + core, pl.ds(k * (FRAMES // 2), FRAMES // 2)]

    def copy(self, ref, k, device):
        remote(ref, ref, self.send, self.recv.at[k], device).start()

    def own(self):
        mine = self.whole(self.x, self.core)
        for first in range(2) if self.split else (None,):
            for way, to in ((0, self.next), (1, self.prev)):
                if first is None:
                    self.copy(mine, way, to)
                else:
                    part = (way + first) % 2
                    self.copy(self.half(self.x, self.core, part), 5 * first + way, to)
        self.copy(mine, 4, self.other)

    def relay(self):
        ways = ((0, NX - 1, self.next), (1, 1, self.prev))
        for way, dx, to in ways:
            came, part = self.whole(self.x + dx, self.core), self.half(self.x + dx, self.core, way)
            wait_on(part if self.split else came, self.recv.at[way])
            self.copy(part, 2 + way, to)
            if not self.split:
                self.copy(came, 4, self.other)
        if self.split:
            for way, dx, to in ways:
                wait_on(self.half(self.x + dx, self.core, 1 - way), self.recv.at[5 + way])
                self.copy(self.whole(self.x + dx, self.core), 4, self.other)

    def relay_far(self):
        for way in range(2):
            came = self.half(self.x + 2, self.core, way)
            wait_on(came, self.recv.at[2 + way])
            self.copy(came, 4, self.other)

    def finish(self):
        wait_on(self.groups.at[pl.ds(0, 4)], self.recv.at[4])

    def drain(self):
        wait_on(self.groups.at[pl.ds(0, 7)], self.send)


def softmax_rows(scores):
    largest = jnp.max(scores, axis=-1, keepdims=True)
    expo = jnp.exp2((scores - largest) * EXP_SCALE)
    return expo.astype(BF16), jnp.sum(expo, axis=-1, keepdims=True)


def dot_t(a, b):
    return lax.dot_general(a, b, (((1,), (1,)), ((), ())), preferred_element_type=F32)


def block_kernel(
    labels,
    q_hbm,
    k_hbm,
    v_hbm,
    w_hbm,
    out,
    table,
    apart,
    heads_in,
    slots,
    got,
    mixed,
    either_spatial,
    either_temporal,
    gathered,
    weight0,
    weight1,
    weight2,
    weight3,
    picked_weight,
    total,
    result,
    load_sem,
    out_sem,
    fwd_send,
    fwd_recv,
    ret_send,
    ret_recv,
    wz_send,
    wz_recv,
    wy_send,
    wy_recv,
    far_recv,
    x_send,
    x_recv,
):
    frame, head = lax.axis_index("frame"), lax.axis_index("head")
    y, z = frame // NZ, frame % NZ
    weight = (weight0, weight1, weight2, weight3)
    x, core = head // 2, head % 2

    load_weight = pltpu.make_async_copy(w_hbm, weight0.at[pl.ds(z * 10, 10)], load_sem.at[0])
    load_weight.start()
    for n, source in enumerate((q_hbm, k_hbm, v_hbm)):
        for h in range(HEAD_DEV):
            pltpu.make_async_copy(
                source.at[:, pl.ds(h * HDIM, HDIM)], heads_in.at[n, h], load_sem.at[1]
            ).start()

    barrier = pltpu.get_barrier_semaphore()

    def greet(k, carry):
        pl.semaphore_signal(
            barrier, inc=1, device_id=((frame + k) % FRAMES, head), device_id_type=MESH
        )
        return carry

    lax.fori_loop(1, FRAMES, greet, 0)
    for there in (((x + 1) % NX) * 2 + core, ((x + NX - 1) % NX) * 2 + core, x * 2 + 1 - core):
        pl.semaphore_signal(barrier, inc=1, device_id=(frame, there), device_id_type=MESH)

    def fill(g, line):
        label = [labels[g * HEAD_DEV + h] for h in range(HEAD_DEV)]
        temporal_count = sum(label)
        rank, ones = [], 0
        for h in range(HEAD_DEV):
            rank.append(label[h] * (HEAD_DEV - temporal_count + ones) + (1 - label[h]) * (h - ones))
            ones = ones + label[h]
        for slot in range(HEAD_DEV):
            table[line * 8 + slot] = sum(
                h * (rank[h] == slot).astype(jnp.int32) for h in range(HEAD_DEV)
            )
        table[line * 8 + HEAD_DEV] = temporal_count - 2

    def fill_all():
        for g in range(GROUPS):
            fill(g, 1 + g)
        row_at = lax.broadcasted_iota(jnp.int32, apart.shape, 0) % HALF
        col_at = lax.broadcasted_iota(jnp.int32, apart.shape, 1) % HALF
        apart[...] = jnp.where(row_at == col_at, 0.0, NEG)

    def pick(slot):
        if slot == SLOT_EITHER:
            wait_on(heads_in, load_sem.at[1])
        for n in range(3):
            slots[slot, n] = heads_in[n, table[slot]].reshape(TILED)

    fill(head, 0)
    load_weight.wait()
    pl.semaphore_wait(barrier, FRAMES - 1 + 3)

    ring = WeightRing(weight, wz_send, wz_recv, wy_send, wy_recv, far_recv.at[0], head, y, z)
    gather = [
        AttendedRing(ref, x_send.at[n], x_recv.at[n], n >= SPLIT_FROM, frame, x, core)
        for n, ref in enumerate(
            [gathered.at[slot] for slot in range(4)] + [gathered.at[4, :, :, h] for h in range(2)]
        )
    ]

    def send_forward(sem, first, last, source, target):
        def one(k, carry):
            to = partner(k, y, z)
            remote(
                source(to), target(frame), fwd_send.at[sem], fwd_recv.at[sem], (to, head)
            ).start()
            return carry

        lax.fori_loop(first, last, one, 0)
        if first == 1:
            pltpu.make_async_copy(source(frame), target(frame), fwd_recv.at[sem]).start()

    def forward(s, part):
        send_forward(
            s,
            max(1, part * 8),
            part * 8 + 8,
            lambda to: slots.at[SENT[s], :, to],
            lambda here: got.at[s, :, here],
        )

    def forward_half(h, part):
        send_forward(
            2 + h,
            max(1, part * 16),
            part * 16 + 16,
            lambda to: slots.at[4, :, to, h],
            lambda here: got.at[2, :, here, h],
        )

    def returned(s):
        return either_temporal if SENT[s] == SLOT_EITHER else gathered.at[SENT[s], head]

    def send_back(sem, source, target):
        def one(k, carry):
            to = partner(k, y, z)
            remote(
                source(to), target(frame), ret_send.at[sem], ret_recv.at[sem], (to, head)
            ).start()
            return carry

        lax.fori_loop(1, FRAMES, one, 0)
        pltpu.make_async_copy(source(frame), target(frame), ret_recv.at[sem]).start()

    def spatial(slot):
        def one(i, carry):
            blocks = pl.ds(i * 8, 8)
            query = slots[slot, 0, blocks].reshape(256, HDIM)
            key, value = (slots[slot, n].reshape(POS, HDIM) for n in (1, 2))
            expo, row_sum = softmax_rows(dot_t(query, key))
            mix = jnp.dot(expo, value, preferred_element_type=F32)
            mix = (mix / row_sum).astype(BF16).reshape(8, 2, HALF, HDIM)
            if slot == SLOT_EITHER:
                either_spatial[blocks] = mix
            else:
                gathered[slot, head, blocks] = mix
            return carry

        lax.fori_loop(0, POS // 256, one, 0)

    def temporal(s, h):
        rows = FRAMES * HALF
        query, key, value = (got[s, n, :, h].reshape(rows, HDIM) for n in range(3))
        expo, row_sum = softmax_rows(dot_t(query, key) + apart[...])
        mix = jnp.dot(expo, value, preferred_element_type=F32)
        mixed[s, :, h] = (mix / row_sum).astype(BF16).reshape(FRAMES, HALF, HDIM)

    def attend_temporal(s):
        wait_on(got.at[s], fwd_recv.at[s])
        for h in range(2):
            temporal(s, h)
        send_back(s, lambda to: mixed.at[s, to], lambda here: returned(s).at[here])

    def attend_temporal_half(h):
        wait_on(got.at[2, :, :, h], fwd_recv.at[2 + h])
        temporal(2, h)
        send_back(
            2 + h, lambda to: mixed.at[2, to, h], lambda here: gathered.at[4, head, here, h]
        )

    def come_back(s):
        wait_on(returned(s), ret_recv.at[s])
        if SENT[s] == SLOT_EITHER:
            is_temporal = jnp.full(TILED, table[HEAD_DEV], jnp.int32) == 1
            gathered[SLOT_EITHER, head] = jnp.where(
                is_temporal, either_temporal[...], either_spatial[...]
            )

    def come_back_half(h):
        wait_on(gathered.at[4, head, :, h], ret_recv.at[2 + h])

    def groups_at(d):
        there = (y + d) % NY
        return [(there * 2 + c, c) for c in range(2)]

    def pick_weight(picks):
        for n, (slot, d, g, c) in enumerate(picks):
            at = (table[(1 + g) * 8 + slot] + c * HEAD_DEV) * 8
            for m in range(8):
                picked_weight[pl.ds(n * HDIM + m * 16, 16), :] = weight[d][at + m]

    def project(unit, part=None):
        taken, offsets = UNITS[unit]
        picks = [(slot, d, g, c) for slot in taken for d in offsets for g, c in groups_at(d)]
        depth = len(picks) * HDIM
        if part != 1:
            pick_weight(picks)

        def one(i, carry):
            at = (pl.ds(i * 8, 8),) if part is None else (pl.ds(i * 16, 16), part)
            left = jnp.concatenate(
                [gathered[(slot, g) + at].reshape(256, HDIM) for slot, d, g, c in picks], axis=1
            )
            sums = jnp.dot(left, picked_weight[:depth, :], preferred_element_type=F32)
            sums = sums.reshape(total[at].shape)
            if unit != 0:
                sums = sums + total[at]
            if taken == (4,):
                result[at] = sums.astype(BF16)
            else:
                total[at] = sums
            return carry

        lax.fori_loop(0, 4 if part is None else 2, one, 0)
        if taken == (4,):
            store(part).start()

    def store(h):
        return pltpu.make_async_copy(result.at[:, h], out.at[:, h], out_sem.at[h])

    acts = {
        "pick": pick,
        "fill": fill_all,
        "zs": ring.send_z,
        "zw": ring.wait_z,
        "ys": ring.send_y,
        "yw": ring.wait_y,
        "yr": ring.relay_y,
        "ye": ring.finish_y,
        "fwd": forward,
        "fwh": forward_half,
        "sp": spatial,
        "tm": attend_temporal,
        "tmh": attend_temporal_half,
        "back": come_back,
        "bkh": come_back_half,
        "xo": lambda n: gather[n].own(),
        "xr": lambda n: gather[n].relay(),
        "xf": lambda n: gather[n].relay_far(),
        "xe": lambda n: gather[n].finish(),
        "mm": project,
    }
    for act, *at in ORDER:
        acts[act](*at)

    for h in range(2):
        store(h).wait()
    ring.drain()
    for each in gather:
        each.drain()
    for s in range(2):
        wait_on(slots.at[SENT[s], :, pl.ds(0, FRAMES - 1)], fwd_send.at[s])
        wait_on(mixed.at[s, pl.ds(0, FRAMES - 1)], ret_send.at[s])
    for h in range(2):
        wait_on(slots.at[4, :, pl.ds(0, FRAMES - 1), h], fwd_send.at[2 + h])
        wait_on(mixed.at[2, pl.ds(0, FRAMES - 1), h], ret_send.at[2 + h])


def per_device(queries, key_states, value_states, out_weight, head_labels):
    any_spec = pl.BlockSpec(memory_space=pl.ANY)
    dma = pltpu.SemaphoreType.DMA
    return pl.pallas_call(
        block_kernel,
        out_shape=pltpu.VMEM((FRAMES, 2, HALF, COLS), BF16),
        in_specs=[pl.BlockSpec(memory_space=pltpu.SMEM)] + [any_spec] * 4,
        out_specs=any_spec,
        scratch_shapes=[
            pltpu.SMEM(((1 + GROUPS) * 8,), jnp.int32),
            pltpu.VMEM((FRAMES * HALF, FRAMES * HALF), F32),
            pltpu.VMEM((3, HEAD_DEV, POS, HDIM), BF16),
            pltpu.VMEM((HEAD_DEV, 3) + TILED, BF16),
            pltpu.VMEM((3, 3) + TILED, BF16),
            pltpu.VMEM((3,) + TILED, BF16),
            pltpu.VMEM(TILED, BF16),
            pltpu.VMEM(TILED, BF16),
            pltpu.VMEM((HEAD_DEV, GROUPS) + TILED, BF16),
            pltpu.VMEM((WROWS * NZ // 16, 16, COLS), BF16),
            pltpu.VMEM((WROWS * NZ // 16, 16, COLS), BF16),
            pltpu.VMEM((WROWS * NZ // 16, 16, COLS), BF16),
            pltpu.VMEM((WROWS * NZ // 16, 16, COLS), BF16),
            pltpu.VMEM((GROUPS * HDIM, COLS), BF16),
            pltpu.VMEM((FRAMES, 2, HALF, COLS), F32),
            pltpu.VMEM((FRAMES, 2, HALF, COLS), BF16),
            dma((2,)),
            dma((2,)),
            dma((4,)),
            dma((4,)),
            dma((4,)),
            dma((4,)),
            dma((2,)),
            dma((2, 4)),
            dma((4,)),
            dma((2, NZ)),
            dma((1,)),
            dma((HEAD_DEV + 1,)),
            dma((HEAD_DEV + 1, 7)),
        ],
        compiler_params=pltpu.CompilerParams(
            collective_id=0, has_side_effects=True, vmem_limit_bytes=56 << 20
        ),
        name="block_kernel",
    )(head_labels, queries, key_states, value_states, out_weight.reshape(10, 16, COLS)).reshape(POS, COLS)


def solution(mesh):
    return jax.shard_map(
        per_device,
        mesh=mesh,
        in_specs=(
            P("frame", "head"),
            P("frame", "head"),
            P("frame", "head"),
            P("frame", "head"),
            P(),
        ),
        out_specs=P("frame", "head"),
        check_vma=False,
    )
```

```python
import functools
import math

import jax
import jax.numpy as jnp
from jax import lax
from jax.experimental import pallas as pl
from jax.experimental.pallas import tpu as pltpu
from jax.sharding import PartitionSpec as P

MESH = pl.DeviceIdType.MESH
BF16 = jnp.bfloat16
F32 = jnp.float32
HDIM = 128
POS = 1024
FRAMES = 32
NY, NZ, NX = 4, 8, 4
GROUPS = 8
HEAD_DEV = 5
PB = POS // FRAMES
WROWS = 160
COLS = 640
EXP_SCALE = HDIM**-0.5 * math.log2(math.e)
NEG = -1e30
SPLIT_FROM = 4
HALF = PB // 2
TILED = (FRAMES, 2, HALF, HDIM)

SLOT_EITHER = 2
SENT = (2, 3, 4)

ORDER = (
    ("zs", 1), ("ys", 0), ("pick", 2), ("fwd", 0, 0), ("fwd", 0, 1), ("pick", 0), ("pick", 1), ("pick", 3),
    ("pick", 4), ("fill",), ("zw", 1), ("zs", 2), ("ys", 1), ("ys", 7), ("fwd", 0, 2), ("fwd", 0, 3),
    ("sp", 0), ("xo", 0), ("yw", 0), ("yr", 0), ("zw", 2), ("ys", 2), ("ys", 6), ("fwd", 1, 0), ("fwd", 1, 1),
    ("zs", 3), ("fwd", 1, 2), ("fwd", 1, 3), ("sp", 1), ("xo", 1), ("yw", 1), ("yr", 1), ("yw", 7), ("yr", 7),
    ("tm", 0), ("sp", 2), ("xr", 0), ("xf", 0), ("yw", 2), ("yr", 2), ("yw", 6), ("yr", 6), ("zw", 3),
    ("ys", 3), ("ys", 5), ("zs", 4), ("fwh", 0, 0), ("xr", 1), ("xf", 1), ("back", 0), ("xo", 2), ("tm", 1),
    ("fwh", 0, 1), ("fwh", 1, 0), ("zw", 4), ("ys", 4), ("fwh", 1, 1), ("xe", 0), ("xe", 1), ("mm", 0),
    ("yw", 3), ("yr", 3), ("xr", 2), ("xf", 2), ("yw", 5), ("yr", 5), ("xe", 2), ("tmh", 0), ("back", 1),
    ("xo", 3), ("yw", 4), ("yr", 4), ("mm", 1), ("tmh", 1), ("xr", 3), ("mm", 2), ("bkh", 0), ("xo", 4),
    ("mm", 3), ("xf", 3), ("ye",), ("mm", 4), ("bkh", 1), ("xo", 5), ("xr", 4), ("xe", 3), ("mm", 5, 0),
    ("mm", 5, 1), ("xr", 5), ("xf", 4), ("xe", 4), ("mm", 6, 0), ("xf", 5), ("xe", 5), ("mm", 6, 1),
)


UNITS = (
    ((0, 1), (0,)),
    ((0, 1), (1,)),
    ((0, 1), (3,)),
    ((2,), (0, 1, 3)),
    ((0, 1, 2), (2,)),
    ((3,), (0, 1, 2, 3)),
    ((4,), (0, 1, 2, 3)),
)


def wait_on(ref, sem):
    pltpu.make_async_copy(ref, ref, sem).wait()


def remote(src, dst, send_sem, recv_sem, device):
    return pltpu.make_async_remote_copy(
        src_ref=src,
        dst_ref=dst,
        send_sem=send_sem,
        recv_sem=recv_sem,
        device_id=device,
        device_id_type=MESH,
    )


def partner(k, y, z):
    turn = (k * 11) % FRAMES
    return ((y + turn // NZ) % NY) * NZ + (z + turn % NZ) % NZ


class WeightRing:
    def __init__(self, rows, zs, zr, ys, yr, far, head, y, z):
        self.rows, self.zs, self.zr, self.ys, self.yr, self.far = rows, zs, zr, ys, yr, far
        self.z = z
        self.z_next = (y * NZ + (z + 1) % NZ, head)
        self.z_prev = (y * NZ + (z + NZ - 1) % NZ, head)
        self.y_next = (((y + 1) % NY) * NZ + z, head)
        self.y_prev = (((y + NY - 1) % NY) * NZ + z, head)

    def block(self, d, dz, half=None):
        unit = ((self.z + dz) % NZ) * 10
        if half is None:
            return self.rows[d].at[pl.ds(unit, 10)]
        return self.rows[d].at[pl.ds(unit + half * 5, 5)]

    def send_z(self, t):
        up = self.block(0, NZ + 1 - t, None if t < 4 else 0)
        down = self.block(0, t - 1, None if t < 4 else 1)
        remote(up, up, self.zs.at[0], self.zr.at[0, t - 1], self.z_next).start()
        remote(down, down, self.zs.at[1], self.zr.at[1, t - 1], self.z_prev).start()

    def wait_z(self, t):
        wait_on(self.block(0, NZ - t, None if t < 4 else 0), self.zr.at[0, t - 1])
        wait_on(self.block(0, t, None if t < 4 else 1), self.zr.at[1, t - 1])

    def send_y(self, dz):
        own = self.block(0, dz)
        remote(own, self.block(3, dz), self.ys.at[0], self.yr.at[0, dz], self.y_next).start()
        remote(own, self.block(1, dz), self.ys.at[1], self.yr.at[1, dz], self.y_prev).start()

    def wait_y(self, dz):
        wait_on(self.block(3, dz), self.yr.at[0, dz])
        wait_on(self.block(1, dz), self.yr.at[1, dz])

    def relay_y(self, dz):
        for way, d, to in ((0, 3, self.y_next), (1, 1, self.y_prev)):
            remote(
                self.block(d, dz, way),
                self.block(2, dz, way),
                self.ys.at[2 + way],
                self.far,
                to,
            ).start()

    def finish_y(self):
        wait_on(self.rows[2], self.far)

    def drain(self):
        for way in range(2):
            wait_on(self.rows[0].at[pl.ds(0, 35)], self.zs.at[way])
            wait_on(self.rows[0], self.ys.at[way])
            wait_on(self.rows[0].at[pl.ds(0, 40)], self.ys.at[2 + way])


class AttendedRing:
    def __init__(self, groups, send, recv, split, frame, x, core):
        self.groups, self.send, self.recv, self.split = groups, send, recv, split
        self.x, self.core = x, core
        self.next = (frame, ((x + 1) % NX) * 2 + core)
        self.prev = (frame, ((x + NX - 1) % NX) * 2 + core)
        self.other = (frame, x * 2 + 1 - core)

    def whole(self, x, core):
        return self.groups.at[(x % NX) * 2 + core]

    def half(self, x, core, k):
        return self.groups.at[(x % NX) * 2 + core, pl.ds(k * (FRAMES // 2), FRAMES // 2)]

    def copy(self, ref, k, device):
        remote(ref, ref, self.send, self.recv.at[k], device).start()

    def own(self):
        mine = self.whole(self.x, self.core)
        for first in range(2) if self.split else (None,):
            for way, to in ((0, self.next), (1, self.prev)):
                if first is None:
                    self.copy(mine, way, to)
                else:
                    part = (way + first) % 2
                    self.copy(self.half(self.x, self.core, part), 5 * first + way, to)
        self.copy(mine, 4, self.other)

    def relay(self):
        ways = ((0, NX - 1, self.next), (1, 1, self.prev))
        for way, dx, to in ways:
            came, part = self.whole(self.x + dx, self.core), self.half(self.x + dx, self.core, way)
            wait_on(part if self.split else came, self.recv.at[way])
            self.copy(part, 2 + way, to)
            if not self.split:
                self.copy(came, 4, self.other)
        if self.split:
            for way, dx, to in ways:
                wait_on(self.half(self.x + dx, self.core, 1 - way), self.recv.at[5 + way])
                self.copy(self.whole(self.x + dx, self.core), 4, self.other)

    def relay_far(self):
        for way in range(2):
            came = self.half(self.x + 2, self.core, way)
            wait_on(came, self.recv.at[2 + way])
            self.copy(came, 4, self.other)

    def finish(self):
        wait_on(self.groups.at[pl.ds(0, 4)], self.recv.at[4])

    def drain(self):
        wait_on(self.groups.at[pl.ds(0, 7)], self.send)


def softmax_rows(scores):
    largest = jnp.max(scores, axis=-1, keepdims=True)
    expo = jnp.exp2((scores - largest) * EXP_SCALE)
    return expo.astype(BF16), jnp.sum(expo, axis=-1, keepdims=True)


def dot_t(a, b):
    return lax.dot_general(a, b, (((1,), (1,)), ((), ())), preferred_element_type=F32)


def block_kernel(
    labels,
    q_hbm,
    k_hbm,
    v_hbm,
    w_hbm,
    out,
    table,
    apart,
    heads_in,
    slots,
    got,
    mixed,
    either_spatial,
    either_temporal,
    gathered,
    weight0,
    weight1,
    weight2,
    weight3,
    picked_weight,
    total,
    result,
    load_sem,
    out_sem,
    fwd_send,
    fwd_recv,
    ret_send,
    ret_recv,
    wz_send,
    wz_recv,
    wy_send,
    wy_recv,
    far_recv,
    x_send,
    x_recv,
):
    frame, head = lax.axis_index("frame"), lax.axis_index("head")
    y, z = frame // NZ, frame % NZ
    weight = (weight0, weight1, weight2, weight3)
    x, core = head // 2, head % 2

    load_weight = pltpu.make_async_copy(w_hbm, weight0.at[pl.ds(z * 10, 10)], load_sem.at[0])
    load_weight.start()
    for n, source in enumerate((q_hbm, k_hbm, v_hbm)):
        for h in range(HEAD_DEV):
            pltpu.make_async_copy(
                source.at[:, pl.ds(h * HDIM, HDIM)], heads_in.at[n, h], load_sem.at[1]
            ).start()

    barrier = pltpu.get_barrier_semaphore()

    def greet(k, carry):
        pl.semaphore_signal(
            barrier, inc=1, device_id=((frame + k) % FRAMES, head), device_id_type=MESH
        )
        return carry

    lax.fori_loop(1, FRAMES, greet, 0)
    for there in (((x + 1) % NX) * 2 + core, ((x + NX - 1) % NX) * 2 + core, x * 2 + 1 - core):
        pl.semaphore_signal(barrier, inc=1, device_id=(frame, there), device_id_type=MESH)

    def fill(g, line):
        label = [labels[g * HEAD_DEV + h] for h in range(HEAD_DEV)]
        temporal_count = sum(label)
        rank, ones = [], 0
        for h in range(HEAD_DEV):
            rank.append(label[h] * (HEAD_DEV - temporal_count + ones) + (1 - label[h]) * (h - ones))
            ones = ones + label[h]
        for slot in range(HEAD_DEV):
            table[line * 8 + slot] = sum(
                h * (rank[h] == slot).astype(jnp.int32) for h in range(HEAD_DEV)
            )
        table[line * 8 + HEAD_DEV] = temporal_count - 2

    def fill_all():
        for g in range(GROUPS):
            fill(g, 1 + g)
        row_at = lax.broadcasted_iota(jnp.int32, apart.shape, 0) % HALF
        col_at = lax.broadcasted_iota(jnp.int32, apart.shape, 1) % HALF
        apart[...] = jnp.where(row_at == col_at, 0.0, NEG)

    def pick(slot):
        if slot == SLOT_EITHER:
            wait_on(heads_in, load_sem.at[1])
        for n in range(3):
            slots[slot, n] = heads_in[n, table[slot]].reshape(TILED)

    fill(head, 0)
    load_weight.wait()
    pl.semaphore_wait(barrier, FRAMES - 1 + 3)

    ring = WeightRing(weight, wz_send, wz_recv, wy_send, wy_recv, far_recv.at[0], head, y, z)
    gather = [
        AttendedRing(ref, x_send.at[n], x_recv.at[n], n >= SPLIT_FROM, frame, x, core)
        for n, ref in enumerate(
            [gathered.at[slot] for slot in range(4)] + [gathered.at[4, :, :, h] for h in range(2)]
        )
    ]

    def send_forward(sem, first, last, source, target):
        def one(k, carry):
            to = partner(k, y, z)
            remote(
                source(to), target(frame), fwd_send.at[sem], fwd_recv.at[sem], (to, head)
            ).start()
            return carry

        lax.fori_loop(first, last, one, 0)
        if first == 1:
            pltpu.make_async_copy(source(frame), target(frame), fwd_recv.at[sem]).start()

    def forward(s, part):
        send_forward(
            s,
            max(1, part * 8),
            part * 8 + 8,
            lambda to: slots.at[SENT[s], :, to],
            lambda here: got.at[s, :, here],
        )

    def forward_half(h, part):
        send_forward(
            2 + h,
            max(1, part * 16),
            part * 16 + 16,
            lambda to: slots.at[4, :, to, h],
            lambda here: got.at[2, :, here, h],
        )

    def returned(s):
        return either_temporal if SENT[s] == SLOT_EITHER else gathered.at[SENT[s], head]

    def send_back(sem, source, target):
        def one(k, carry):
            to = partner(k, y, z)
            remote(
                source(to), target(frame), ret_send.at[sem], ret_recv.at[sem], (to, head)
            ).start()
            return carry

        lax.fori_loop(1, FRAMES, one, 0)
        pltpu.make_async_copy(source(frame), target(frame), ret_recv.at[sem]).start()

    def spatial(slot):
        def one(i, carry):
            blocks = pl.ds(i * 8, 8)
            query = slots[slot, 0, blocks].reshape(256, HDIM)
            key, value = (slots[slot, n].reshape(POS, HDIM) for n in (1, 2))
            expo, row_sum = softmax_rows(dot_t(query, key))
            mix = jnp.dot(expo, value, preferred_element_type=F32)
            mix = (mix / row_sum).astype(BF16).reshape(8, 2, HALF, HDIM)
            if slot == SLOT_EITHER:
                either_spatial[blocks] = mix
            else:
                gathered[slot, head, blocks] = mix
            return carry

        lax.fori_loop(0, POS // 256, one, 0)

    def temporal(s, h):
        rows = FRAMES * HALF
        query, key, value = (got[s, n, :, h].reshape(rows, HDIM) for n in range(3))
        expo, row_sum = softmax_rows(dot_t(query, key) + apart[...])
        mix = jnp.dot(expo, value, preferred_element_type=F32)
        mixed[s, :, h] = (mix / row_sum).astype(BF16).reshape(FRAMES, HALF, HDIM)

    def attend_temporal(s):
        wait_on(got.at[s], fwd_recv.at[s])
        for h in range(2):
            temporal(s, h)
        send_back(s, lambda to: mixed.at[s, to], lambda here: returned(s).at[here])

    def attend_temporal_half(h):
        wait_on(got.at[2, :, :, h], fwd_recv.at[2 + h])
        temporal(2, h)
        send_back(
            2 + h, lambda to: mixed.at[2, to, h], lambda here: gathered.at[4, head, here, h]
        )

    def come_back(s):
        wait_on(returned(s), ret_recv.at[s])
        if SENT[s] == SLOT_EITHER:
            is_temporal = jnp.full(TILED, table[HEAD_DEV], jnp.int32) == 1
            gathered[SLOT_EITHER, head] = jnp.where(
                is_temporal, either_temporal[...], either_spatial[...]
            )

    def come_back_half(h):
        wait_on(gathered.at[4, head, :, h], ret_recv.at[2 + h])

    def groups_at(d):
        there = (y + d) % NY
        return [(there * 2 + c, c) for c in range(2)]

    def pick_weight(picks):
        for n, (slot, d, g, c) in enumerate(picks):
            at = (table[(1 + g) * 8 + slot] + c * HEAD_DEV) * 8
            for m in range(8):
                picked_weight[pl.ds(n * HDIM + m * 16, 16), :] = weight[d][at + m]

    def project(unit, part=None):
        taken, offsets = UNITS[unit]
        picks = [(slot, d, g, c) for slot in taken for d in offsets for g, c in groups_at(d)]
        depth = len(picks) * HDIM
        if part != 1:
            pick_weight(picks)

        def one(i, carry):
            at = (pl.ds(i * 8, 8),) if part is None else (pl.ds(i * 16, 16), part)
            left = jnp.concatenate(
                [gathered[(slot, g) + at].reshape(256, HDIM) for slot, d, g, c in picks], axis=1
            )
            sums = jnp.dot(left, picked_weight[:depth, :], preferred_element_type=F32)
            sums = sums.reshape(total[at].shape)
            if unit != 0:
                sums = sums + total[at]
            if taken == (4,):
                result[at] = sums.astype(BF16)
            else:
                total[at] = sums
            return carry

        lax.fori_loop(0, 4 if part is None else 2, one, 0)
        if taken == (4,):
            store(part).start()

    def store(h):
        return pltpu.make_async_copy(result.at[:, h], out.at[:, h], out_sem.at[h])

    acts = {
        "pick": pick,
        "fill": fill_all,
        "zs": ring.send_z,
        "zw": ring.wait_z,
        "ys": ring.send_y,
        "yw": ring.wait_y,
        "yr": ring.relay_y,
        "ye": ring.finish_y,
        "fwd": forward,
        "fwh": forward_half,
        "sp": spatial,
        "tm": attend_temporal,
        "tmh": attend_temporal_half,
        "back": come_back,
        "bkh": come_back_half,
        "xo": lambda n: gather[n].own(),
        "xr": lambda n: gather[n].relay(),
        "xf": lambda n: gather[n].relay_far(),
        "xe": lambda n: gather[n].finish(),
        "mm": project,
    }
    for act, *at in ORDER:
        acts[act](*at)

    for h in range(2):
        store(h).wait()
    ring.drain()
    for each in gather:
        each.drain()
    for s in range(2):
        wait_on(slots.at[SENT[s], :, pl.ds(0, FRAMES - 1)], fwd_send.at[s])
        wait_on(mixed.at[s, pl.ds(0, FRAMES - 1)], ret_send.at[s])
    for h in range(2):
        wait_on(slots.at[4, :, pl.ds(0, FRAMES - 1), h], fwd_send.at[2 + h])
        wait_on(mixed.at[2, pl.ds(0, FRAMES - 1), h], ret_send.at[2 + h])


def per_device(queries, key_states, value_states, out_weight, head_labels):
    any_spec = pl.BlockSpec(memory_space=pl.ANY)
    dma = pltpu.SemaphoreType.DMA
    return pl.pallas_call(
        block_kernel,
        out_shape=pltpu.VMEM((FRAMES, 2, HALF, COLS), BF16),
        in_specs=[pl.BlockSpec(memory_space=pltpu.SMEM)] + [any_spec] * 4,
        out_specs=any_spec,
        scratch_shapes=[
            pltpu.SMEM(((1 + GROUPS) * 8,), jnp.int32),
            pltpu.VMEM((FRAMES * HALF, FRAMES * HALF), F32),
            pltpu.VMEM((3, HEAD_DEV, POS, HDIM), BF16),
            pltpu.VMEM((HEAD_DEV, 3) + TILED, BF16),
            pltpu.VMEM((3, 3) + TILED, BF16),
            pltpu.VMEM((3,) + TILED, BF16),
            pltpu.VMEM(TILED, BF16),
            pltpu.VMEM(TILED, BF16),
            pltpu.VMEM((HEAD_DEV, GROUPS) + TILED, BF16),
            pltpu.VMEM((WROWS * NZ // 16, 16, COLS), BF16),
            pltpu.VMEM((WROWS * NZ // 16, 16, COLS), BF16),
            pltpu.VMEM((WROWS * NZ // 16, 16, COLS), BF16),
            pltpu.VMEM((WROWS * NZ // 16, 16, COLS), BF16),
            pltpu.VMEM((GROUPS * HDIM, COLS), BF16),
            pltpu.VMEM((FRAMES, 2, HALF, COLS), F32),
            pltpu.VMEM((FRAMES, 2, HALF, COLS), BF16),
            dma((2,)),
            dma((2,)),
            dma((4,)),
            dma((4,)),
            dma((4,)),
            dma((4,)),
            dma((2,)),
            dma((2, 4)),
            dma((4,)),
            dma((2, NZ)),
            dma((1,)),
            dma((HEAD_DEV + 1,)),
            dma((HEAD_DEV + 1, 7)),
        ],
        compiler_params=pltpu.CompilerParams(
            collective_id=0, has_side_effects=True, vmem_limit_bytes=56 << 20
        ),
        name="block_kernel",
    )(head_labels, queries, key_states, value_states, out_weight.reshape(10, 16, COLS)).reshape(POS, COLS)


def solution(mesh):
    return jax.shard_map(
        per_device,
        mesh=mesh,
        in_specs=(
            P("frame", "head"),
            P("frame", "head"),
            P("frame", "head"),
            P("frame", "head"),
            P(),
        ),
        out_specs=P("frame", "head"),
        check_vma=False,
    )
```
